32 devices in a mesh: dp: 4 (over y, x), fsdp: 8 (over z, core).
Axes of the slice: x: 2, y: 2, z: 4, core: 2. Of those that a mesh axis runs over, the one named last changes fastest.
Arguments:
- features: bfloat16 [4096, 640], P(('dp', 'fsdp')), may hold values from -6 to 6
- heights: int32 [32, 4], P(('dp', 'fsdp')), may hold values from 0 to 32, as said below
- widths: int32 [32, 4], P(('dp', 'fsdp')), may hold values from 0 to 32, as said below
- timesteps: int32 [32, 4], P(('dp', 'fsdp')), may hold values from 0 to 999
- norm_gain: float32 [640], replicated, may hold values from 0.1 to 1.9
- norm_shift: float32 [640], replicated, may hold values from -3 to 3
- conv_weight: bfloat16 [768, 5760], P('fsdp'), may hold values from -0.078125 to 0.078125
- time_weight: bfloat16 [768, 320], P('fsdp'), may hold values from -0.3125 to 0.3125
- cotangent: bfloat16 [4096, 768], P(('dp', 'fsdp')), may hold values from -6 to 6
Outputs:
- block_out: bfloat16 [4096, 768], P(('dp', 'fsdp'))
- grad_features: bfloat16 [4096, 640], P(('dp', 'fsdp'))
- grad_conv: float32 [768, 5760], P('fsdp')
- grad_time: float32 [768, 320], P('fsdp')
- grad_gain: float32 [640], replicated
- grad_shift: float32 [640], replicated
The draws below stay inside these ranges and needn't reach their ends.
Inputs may be any that keep to these rules, and one draw needn't show every extreme that they name: In each block the live pixels heights * widths sum to at most 128, and in some block to exactly 128; every block has one or more images, slot after slot; an empty slot has height and width 0; sides are powers of two. `widths`: as for heights; a live image has width 2 or more.
All inputs are finite; a program needn't handle non-finite values.
Results may differ from the reference program's by a relative error of at most 0.0045.
Values may be sent and summed in bfloat16 or wider, within the bound.
No kernel may reach another device: no remote copies, remote signals or barrier semaphores. Data moves between devices by JAX's collectives and lax.ppermute only.
A program may use at most 128 MiB of HBM per device.

```python
import math
import jax
import jax.numpy as jnp
from jax import lax

C = 640
CO = 768
FREQ = 320
GROUPS = 32
IMG_DEV = 4
P_CAP = 128
SHARDS = 32
ROWS = 4096


def bucket_shapes(key):
    log_cap = P_CAP.bit_length() - 1
    keys = jax.random.split(jax.random.fold_in(key, 7), 5)
    count = jax.random.randint(keys[0], (SHARDS,), 1, IMG_DEV + 1)
    fullest = jax.random.randint(keys[1], (), 0, SHARDS)
    second = (fullest + 1) % SHARDS
    shard_ids = jnp.arange(SHARDS)
    is_tall = shard_ids == fullest
    is_wide = shard_ids == second
    is_full = is_tall | is_wide
    count = jnp.where(is_full, 1, count)
    log_share = jnp.array([0, 0, 1, 2, 2], jnp.int32)[jnp.minimum(count, 4)]
    top = log_cap - log_share
    lower = jax.random.randint(keys[3], (SHARDS, IMG_DEV), 0, 3)
    level = jnp.where(is_full[:, None], top[:, None], jnp.maximum(2, top[:, None] - lower))
    bottom = jnp.maximum(1, level - 5)
    ceiling = jnp.minimum(5, level - 1)
    chosen = jax.random.randint(keys[4], (SHARDS, IMG_DEV), 0, 5)
    exponent = bottom + chosen % (ceiling - bottom + 1)
    exponent = jnp.where(is_tall[:, None], ceiling, exponent)
    exponent = jnp.where(is_wide[:, None], bottom, exponent)
    used = jnp.arange(IMG_DEV)[None, :] < count[:, None]
    heights = jnp.where(used, jnp.left_shift(1, exponent), 0)
    widths = jnp.where(used, jnp.left_shift(1, level - exponent), 0)
    return (heights.astype(jnp.int32), widths.astype(jnp.int32))


def draw_heights(key, part):
    return bucket_shapes(key)[0]


def draw_widths(key, part):
    return bucket_shapes(key)[1]


def touch_ends(drawn, own_key, low, high):
    longest = drawn.shape.index(max(drawn.shape))
    spots = []
    for shift in (0, 1):
        where = [jax.random.randint(jax.random.fold_in(own_key, axis), (), 0, length) for axis, length in enumerate(drawn.shape)]
        where[longest] = (where[longest] + shift) % drawn.shape[longest]
        spots.append(tuple(where))
    return drawn.at[spots[0]].set(low).at[spots[1]].set(high)


def block_scale(key, shape, shards, smallest, top_value):
    gain, own = 1.0, jax.random.fold_in(key, 6)
    for dim, parts in shards:
        steps = jnp.exp(jax.random.uniform(jax.random.fold_in(own, dim), (parts,), jnp.float32, smallest / len(shards), top_value / len(shards)))
        gain = gain * jnp.repeat(steps, shape[dim] // parts).reshape([-1 if axis == dim else 1 for axis in range(len(shape))])
    return gain


def gaussian(stream_key, extent, scale, reach, pieces=(), held_as=jnp.bfloat16):
    values = scale * jax.random.normal(stream_key, extent, jnp.float32)
    if pieces:
        values = values * block_scale(stream_key, extent, pieces, -0.22, 0.18)
    return jnp.clip(values, -reach, reach).astype(held_as)


def setup_inputs(seed: int = 0) -> dict:
    streams_of = jax.random.split(jax.random.key(seed), 10)
    features = gaussian(streams_of[0], (ROWS, C), 1.0, 6.0, ((0, 32),))
    heights = draw_heights(jax.random.fold_in(streams_of[9], 71), 0)
    widths = draw_widths(jax.random.fold_in(streams_of[9], 71), 0)
    timesteps = touch_ends(jax.random.randint(streams_of[3], (SHARDS, IMG_DEV), 0, 1000), jax.random.fold_in(streams_of[3], 1), 0, 999).astype(jnp.int32)
    norm_gain = jnp.clip(1.0 + 0.18 * jax.random.normal(streams_of[4], (C,), jnp.float32), 0.1, 1.9)
    norm_shift = gaussian(streams_of[5], (C,), 0.5, 3.0, (), jnp.float32)
    conv_weight = gaussian(streams_of[6], (CO, 9 * C), (9 * C) ** -0.5, 0.078125, ((0, 8),))
    time_weight = gaussian(streams_of[7], (CO, FREQ), FREQ ** -0.5, 0.3125, ((0, 8),))
    cotangent = gaussian(streams_of[8], (ROWS, CO), 1.0, 6.0, ((0, 32),))
    return {"features": features, "heights": heights, "widths": widths, "timesteps": timesteps, "norm_gain": norm_gain, "norm_shift": norm_shift, "conv_weight": conv_weight, "time_weight": time_weight, "cotangent": cotangent}


highest = lax.Precision.HIGHEST

def layout(heights_row, widths_row, rows):
    images = heights_row.shape[0]
    area = (heights_row * widths_row).astype(jnp.int32)
    ends = jnp.cumsum(area).astype(jnp.int32)
    starts = (ends - area).astype(jnp.int32)
    position = jnp.arange(rows, dtype=jnp.int32)
    image = lax.optimization_barrier(jnp.sum((position[:, None] >= ends[None, :]).astype(jnp.int32), axis=1))
    live = position < ends[images - 1]
    member = (image[:, None] == jnp.arange(images, dtype=jnp.int32)[None, :]) & live[:, None]
    first = lax.optimization_barrier(jnp.sum(jnp.where(member, starts[None, :], 0), axis=1)).astype(jnp.int32)
    height = lax.optimization_barrier(jnp.sum(jnp.where(member, heights_row[None, :], 0), axis=1)).astype(jnp.int32)
    width = lax.optimization_barrier(jnp.sum(jnp.where(member, widths_row[None, :], 0), axis=1)).astype(jnp.int32)
    offset = position - first
    width_safe = jnp.maximum(width, 1)
    row_index = offset // width_safe
    column = offset - row_index * width_safe
    targets = []
    for shift_row in (-1, 0, 1):
        for shift_col in (-1, 0, 1):
            near_row = row_index + shift_row
            near_col = column + shift_col
            valid = live & (near_row >= 0) & (near_row < height) & (near_col >= 0) & (near_col < width)
            targets.append(jnp.where(valid, first + near_row * width + near_col, rows).astype(jnp.int32))
    neighbours = jnp.stack(targets, axis=1).astype(jnp.int32)
    return (neighbours, live, member.astype(jnp.float32))

def timestep_features(times_row, feature_count):
    half = feature_count // 2
    rates = jnp.exp(-math.log(10000.0) * jnp.arange(half, dtype=jnp.float32) / half)
    angles = times_row.astype(jnp.float32)[:, None] * rates[None, :]
    return jnp.concatenate([jnp.sin(angles), jnp.cos(angles)], axis=1).astype(jnp.bfloat16)

def group_mean(values, member, counts):
    sums = jnp.dot(member.T, values, precision=highest)
    images, channels = sums.shape
    grouped = lax.optimization_barrier(jnp.sum(sums.reshape(images, GROUPS, channels // GROUPS), axis=2)) / counts[:, None]
    spread = jnp.repeat(grouped, channels // GROUPS, axis=1)
    return jnp.dot(member, spread, precision=highest)

def prepare(features, heights_row, widths_row, norm_gain, norm_shift, cotangent):
    rows, channels = features.shape
    neighbours, live, member = layout(heights_row, widths_row, rows)
    counts = jnp.maximum((heights_row * widths_row).astype(jnp.float32) * (channels // GROUPS), 1.0)
    values = features.astype(jnp.float32)
    mean = group_mean(values, member, counts)
    centered = values - mean
    variance = group_mean(centered * centered, member, counts)
    inverse_std = lax.rsqrt(variance + 1e-05) * live[:, None].astype(jnp.float32)
    normed = centered * inverse_std
    shifted = normed * norm_gain[None, :] + norm_shift[None, :]
    activated = (shifted * jax.nn.sigmoid(shifted)).astype(jnp.bfloat16)
    padded = jnp.concatenate([activated, jnp.zeros((1, channels), jnp.bfloat16)], axis=0)
    patches = padded[neighbours].reshape(rows, 9 * channels)
    cotan_live = jnp.where(live[:, None], cotangent, jnp.zeros_like(cotangent))
    cotan_padded = jnp.concatenate([cotan_live, jnp.zeros((1, cotangent.shape[1]), jnp.bfloat16)], axis=0)
    return (neighbours, live, member, counts, normed, shifted, inverse_std, patches, cotan_live, cotan_padded)

def finish(grad_act, shifted, normed, inverse_std, member, counts, norm_gain, scale):
    sigmoid_value = jax.nn.sigmoid(shifted)
    grad_shifted = grad_act * sigmoid_value * (1.0 + shifted * (1.0 - sigmoid_value))
    gain_term = lax.optimization_barrier(jnp.sum(grad_shifted * normed, axis=0)) * scale
    shift_term = lax.optimization_barrier(jnp.sum(grad_shifted, axis=0)) * scale
    grad_normed = grad_shifted * norm_gain[None, :]
    mean_grad = group_mean(grad_normed, member, counts)
    mean_cross = group_mean(grad_normed * normed, member, counts)
    grad_features = (inverse_std * (grad_normed - mean_grad - normed * mean_cross)).astype(jnp.bfloat16)
    return (grad_features, gain_term, shift_term)

def reference(features, heights, widths, timesteps, norm_gain, norm_shift, conv_weight, time_weight, cotangent):
    scale = 1.0 / math.sqrt(SHARDS * P_CAP)
    channels = features.shape[1]
    out_channels = conv_weight.shape[0]
    blocks = (features.reshape(SHARDS, P_CAP, channels), heights, widths, timesteps, cotangent.reshape(SHARDS, P_CAP, out_channels))

    def one_shard(carry, block):
        feature_block, heights_row, widths_row, times_row, cotan_block = block
        neighbours, live, member, counts, normed, shifted, inverse_std, patches, cotan_live, cotan_padded = prepare(feature_block, heights_row, widths_row, norm_gain, norm_shift, cotan_block)
        embed = timestep_features(times_row, FREQ)
        bias_image = lax.dot_general(embed, time_weight, (((1,), (1,)), ((), ())), preferred_element_type=jnp.float32)
        bias_rows = jnp.dot(member, bias_image, precision=highest)
        before = lax.dot_general(patches, conv_weight, (((1,), (1,)), ((), ())), preferred_element_type=jnp.float32) + bias_rows
        block_out = jnp.where(live[:, None], before, 0.0).astype(jnp.bfloat16)
        grad_act = jnp.zeros((P_CAP, channels), jnp.float32)
        for tap in range(9):
            gathered = cotan_padded[neighbours[:, 8 - tap]]
            grad_act = grad_act + jnp.dot(gathered, conv_weight[:, tap * channels:(tap + 1) * channels], preferred_element_type=jnp.float32)
        conv_term = lax.dot_general(cotan_live, patches, (((0,), (0,)), ((), ())), preferred_element_type=jnp.float32) * scale
        per_image = jnp.dot(member.T, cotan_live.astype(jnp.float32), precision=highest)
        time_term = lax.dot_general(per_image, embed.astype(jnp.float32), (((0,), (0,)), ((), ())), precision=highest) * scale
        grad_features, gain_term, shift_term = finish(grad_act, shifted, normed, inverse_std, member, counts, norm_gain, scale)
        carry = (carry[0] + conv_term, carry[1] + time_term, carry[2] + gain_term, carry[3] + shift_term)
        return (carry, (block_out, grad_features))
    start = (jnp.zeros((out_channels, 9 * channels), jnp.float32), jnp.zeros((out_channels, FREQ), jnp.float32), jnp.zeros((channels,), jnp.float32), jnp.zeros((channels,), jnp.float32))
    totals, stacked = lax.scan(one_shard, start, blocks)
    block_out = stacked[0].reshape(SHARDS * P_CAP, out_channels)
    grad_features = stacked[1].reshape(SHARDS * P_CAP, channels)
    return (block_out, grad_features, totals[0], totals[1], totals[2], totals[3])
```

```python
import functools
import math

import jax
import jax.numpy as jnp
from jax import lax
from jax.experimental import pallas as pl
from jax.experimental.pallas import tpu as pltpu
from jax.sharding import PartitionSpec as P

GROUPS = 32
IMAGES = 4
LANES = 128
VMEM_BYTES = 56 * 1024 * 1024

bf16 = jnp.bfloat16
f32 = jnp.float32


def dot(a, b, dims=((1,), (0,))):
    return lax.dot_general(a, b, (dims, ((), ())), preferred_element_type=f32)


def split3(x):
    hi = x.astype(bf16)
    rest = x - hi.astype(f32)
    mid = rest.astype(bf16)
    low = (rest - mid.astype(f32)).astype(bf16)
    return hi, mid, low


def exact_dot(x, ones):
    rows = x.shape[0]
    out = dot(jnp.concatenate(split3(x), axis=0), ones)
    return out[:rows] + out[rows : 2 * rows] + out[2 * rows :]


def image_bounds(meta_ref, source):
    start = jnp.int32(0)
    found = []
    for j in range(IMAGES):
        height = meta_ref[source, j]
        width = meta_ref[source, IMAGES + j]
        area = height * width
        found.append((start, start + area, width, area))
        start = start + area
    return found


def inverse_area(area):
    return 1.0 / jnp.maximum(area, 1).astype(f32)


def masks(bounds, shape):
    row = lax.broadcasted_iota(jnp.int32, shape, 0)
    return [(row >= start) & (row < end) for start, end, _, _ in bounds]


def spread(members, table, shape):
    out = jnp.zeros(shape, f32)
    for j in range(IMAGES):
        out = jnp.where(members[j], table[j : j + 1, :], out)
    return out


def image_sums(members, values, bounds):
    sums = []
    for j in range(IMAGES):
        total = jnp.sum(jnp.where(members[j], values, 0.0), axis=0, keepdims=True)
        sums.append(total * inverse_area(bounds[j][3]))
    return jnp.concatenate(sums, axis=0)


def tap_matrices(bounds, rows):
    shape = (rows, rows)
    row = lax.broadcasted_iota(jnp.int32, shape, 0)
    gap = lax.broadcasted_iota(jnp.int32, shape, 1) - row
    width = jnp.zeros(shape, jnp.int32)
    area = jnp.zeros(shape, jnp.int32)
    first = jnp.zeros(shape, jnp.int32)
    for start, end, wide, size in bounds:
        member = (row >= start) & (row < end)
        width = jnp.where(member, wide, width)
        area = jnp.where(member, size, area)
        first = jnp.where(member, start, first)
    offset = row - first
    column = offset & (width - 1)
    columns = {-1: column >= 1, 0: column >= 0, 1: column + 1 < width}
    taps = []
    for shift_row in (-1, 0, 1):
        moved = offset + shift_row * width
        inside = (moved >= 0) & (moved < area)
        left = gap - shift_row * width
        for shift_col in (-1, 0, 1):
            hit = inside & columns[shift_col] & (left == shift_col)
            taps.append(jnp.where(hit, 1.0, 0.0).astype(bf16))
    return taps


def weight_grad_kernel(
    count,
    low_taps,
    source_ref,
    meta_ref,
    *refs,
):
    features = refs[:count]
    (
        cotan_ref,
        embed_ref,
        same_ref,
        gain_ref,
        shift_ref,
        low_ref,
        high_ref,
        act_ref,
        normed_ref,
        rstd_ref,
        taps_ref,
        stats,
        sums,
        turned,
    ) = refs[count:]
    rows, channels = features[0].shape
    owned = cotan_ref.shape[2]
    padded = turned.shape[0] // 9
    group_size = channels // GROUPS
    same = same_ref[...]
    for b in range(count):
        bounds = image_bounds(meta_ref, source_ref[b])
        members = masks(bounds, (rows, channels))
        stats[b * IMAGES : (b + 1) * IMAGES, :] = image_sums(
            members, features[b][...].astype(f32), bounds
        )
    means = exact_dot(stats[...], same) * (1.0 / group_size)
    for b in range(count):
        bounds = image_bounds(meta_ref, source_ref[b])
        members = masks(bounds, (rows, channels))
        mean = spread(members, means[b * IMAGES : (b + 1) * IMAGES], (rows, channels))
        centered = features[b][...].astype(f32) - mean
        normed_ref[b] = centered
        stats[b * IMAGES : (b + 1) * IMAGES, :] = image_sums(members, centered * centered, bounds)
    variance = exact_dot(stats[...], same) * (1.0 / group_size)
    rstds = lax.rsqrt(variance + 1e-05)
    gain = gain_ref[...]
    shift = shift_ref[...]
    for b in range(count):
        source = source_ref[b]
        bounds = image_bounds(meta_ref, source)
        members = masks(bounds, (rows, channels))
        rstd = spread(members, rstds[b * IMAGES : (b + 1) * IMAGES], (rows, channels))
        if b == 0:
            rstd_ref[...] = rstd
        normed = normed_ref[b] * rstd
        normed_ref[b] = normed
        shifted = normed * gain + shift
        act_ref[b * rows : (b + 1) * rows, :] = (shifted * jax.nn.sigmoid(shifted)).astype(bf16)

        taps = jnp.concatenate(tap_matrices(bounds, rows), axis=1)
        taps_ref[b] = taps
        cotan = cotan_ref[source, :rows, :]
        wide = cotan.astype(f32)
        if owned < LANES:
            wide = jnp.concatenate([wide, jnp.zeros((rows, LANES - owned), f32)], axis=1)
        moved = dot(wide.T.astype(bf16), taps).astype(bf16)
        for t in range(9):
            turned[t * padded : (t + 1) * padded, b * rows : (b + 1) * rows] = moved[
                :padded, t * rows : (t + 1) * rows
            ]
        image = lax.broadcasted_iota(jnp.int32, (2 * IMAGES, rows), 0)
        place = lax.broadcasted_iota(jnp.int32, (2 * IMAGES, rows), 1)
        member = jnp.zeros((2 * IMAGES, rows), f32)
        for j in range(IMAGES):
            start, end, _, _ = bounds[j]
            member = jnp.where((image == j) & (place >= start) & (place < end), 1.0, member)
        sums[source] = dot(member.astype(bf16), cotan)
    grad = dot(turned[...], act_ref[...])
    for t in range(9):
        part = grad[t * padded : t * padded + owned].astype(bf16)
        if t < low_taps:
            low_ref[:, t * channels : (t + 1) * channels] = part
        else:
            high_ref[:, (t - low_taps) * channels : (t - low_taps + 1) * channels] = part
    totals = jnp.concatenate([sums[s] for s in range(count)], axis=0)
    embed = embed_ref[...]
    time_grad = jnp.zeros((owned, embed.shape[1]), f32)
    for term in split3(totals):
        time_grad = time_grad + dot(term, embed, ((0,), (0,)))
    spare = low_ref.shape[1] - low_taps * channels - embed.shape[1]
    low_ref[:, low_taps * channels :] = jnp.concatenate(
        [time_grad, jnp.zeros((owned, spare), f32)], axis=1
    ).astype(bf16)


def conv_kernel(
    count,
    source_ref,
    meta_ref,
    act_ref,
    normed_ref,
    taps_ref,
    cotan_ref,
    embed_ref,
    conv_ref,
    time_ref,
    gain_ref,
    shift_ref,
    out_ref,
    own_ref,
    other_ref,
    terms_ref,
    weights,
    biases,
    moved,
    product,
):
    _, rows, channels = normed_ref.shape
    owned = cotan_ref.shape[2]
    weights[...] = jnp.zeros_like(weights)
    for t in range(9):
        weights[t * LANES : t * LANES + owned, :] = conv_ref[:, t * channels : (t + 1) * channels]
    bias = dot(embed_ref[...], time_ref[...], ((1,), (1,)))
    for s in range(count):
        biases[s] = bias[s * 2 * IMAGES : (s + 1) * 2 * IMAGES]
    gain = gain_ref[...]
    shift = shift_ref[...]
    gain_term = jnp.zeros((1, channels), f32)
    shift_term = jnp.zeros((1, channels), f32)
    for b in range(count):
        taps = taps_ref[b]
        stacked = jnp.concatenate([taps[:, (8 - t) * rows : (9 - t) * rows] for t in range(9)], axis=0)
        cotan = cotan_ref[source_ref[b], :rows, :]
        if owned < LANES:
            cotan = jnp.concatenate([cotan, jnp.zeros((rows, LANES - owned), bf16)], axis=1)
        shifted_cotan = dot(stacked, cotan).astype(bf16)
        for t in range(9):
            moved[b * rows : (b + 1) * rows, t * LANES : (t + 1) * LANES] = shifted_cotan[
                t * rows : (t + 1) * rows
            ]
    for pair in range(count // 2):
        grad_act = dot(moved[2 * pair * rows : 2 * (pair + 1) * rows, :], weights[...])
        own_ref[pair] = grad_act[:rows].astype(bf16)
        other_ref[pair] = grad_act[rows:].astype(bf16)
        normed = normed_ref[2 * pair : 2 * pair + 2].reshape(2 * rows, channels)
        shifted = normed * gain + shift
        sig = jax.nn.sigmoid(shifted)
        slope = grad_act * (sig * (1.0 + shifted * (1.0 - sig)))
        gain_term = gain_term + jnp.sum(slope * normed, axis=0, keepdims=True)
        shift_term = shift_term + jnp.sum(slope, axis=0, keepdims=True)
        product[...] = dot(
            act_ref[2 * pair * rows : 2 * (pair + 1) * rows, :], weights[...], ((1,), (1,))
        )
        for half in range(2):
            b = 2 * pair + half
            source = source_ref[b]
            values = product[half * rows : (half + 1) * rows, :]
            high = values.astype(bf16)
            low = (values - high.astype(f32)).astype(bf16)
            tiles = [high[:, t * LANES : (t + 1) * LANES] for t in range(9)]
            tiles += [low[:, t * LANES : (t + 1) * LANES] for t in range(9)]
            taps = taps_ref[b]
            total = dot(
                jnp.concatenate([taps, taps], axis=1), jnp.concatenate(tiles, axis=0)
            )[:, :owned]
            bounds = image_bounds(meta_ref, source)
            members = masks(bounds, (rows, owned))
            total = total + spread(members, biases[source], (rows, owned))
            out_ref[source] = total.astype(bf16)
    terms_ref[...] = jnp.concatenate(
        [gain_term, shift_term, jnp.zeros((6, channels), f32)], axis=0
    )


def norm_grad_kernel(
    source_ref, meta_ref, grad_ref, normed_ref, rstd_ref, same_ref, gain_ref, shift_ref, out_ref
):
    rows, channels = grad_ref.shape
    group_size = channels // GROUPS
    normed = normed_ref[0]
    gain = gain_ref[...]
    shifted = normed * gain + shift_ref[...]
    sig = jax.nn.sigmoid(shifted)
    grad = grad_ref[...] * (sig * (1.0 + shifted * (1.0 - sig))) * gain
    bounds = image_bounds(meta_ref, source_ref[0])
    members = masks(bounds, (rows, channels))
    sums = jnp.concatenate(
        [image_sums(members, grad, bounds), image_sums(members, grad * normed, bounds)], axis=0
    )
    means = exact_dot(sums, same_ref[...]) * (1.0 / group_size)
    mean_grad = spread(members, means[:IMAGES], (rows, channels))
    mean_cross = spread(members, means[IMAGES:], (rows, channels))
    out_ref[...] = (rstd_ref[...] * (grad - mean_grad - normed * mean_cross)).astype(bf16)


def call(kernel, outs, scratch, flops, *args):
    smem = pl.BlockSpec(memory_space=pltpu.SMEM)
    vmem = pl.BlockSpec(memory_space=pltpu.VMEM)
    return pl.pallas_call(
        kernel,
        out_shape=outs,
        in_specs=[smem, smem] + [vmem] * (len(args) - 2),
        out_specs=jax.tree.map(lambda _: vmem, outs),
        scratch_shapes=scratch,
        compiler_params=pltpu.CompilerParams(vmem_limit_bytes=VMEM_BYTES),
        cost_estimate=pl.CostEstimate(flops=flops, bytes_accessed=8 << 20, transcendentals=0),
    )(*args)


def exchange(value, axis, bit):
    size = lax.axis_size(axis)
    return lax.ppermute(value, axis, [(i, i ^ bit) for i in range(size)])


def timestep_features(times, feature_count):
    half = feature_count // 2
    rates = jnp.exp(-math.log(10000.0) * jnp.arange(half, dtype=f32) / half)
    angles = times.astype(f32)[..., None] * rates
    return jnp.concatenate([jnp.sin(angles), jnp.cos(angles)], axis=-1).astype(bf16)


def shards(
    features, heights, widths, timesteps, norm_gain, norm_shift, conv_weight, time_weight, cotangent
):
    rows, channels = features.shape
    replicas = lax.axis_size("dp")
    holders = lax.axis_size("fsdp")
    chips = holders // 2
    owned = conv_weight.shape[0]
    out_channels = cotangent.shape[1]
    feature_count = time_weight.shape[1]
    scale = 1.0 / math.sqrt(replicas * holders * rows)
    me = lax.axis_index("fsdp")

    near = [features] + [exchange(features, "fsdp", 2 * k) for k in range(1, chips)]
    far = [exchange(block, "fsdp", 1) for block in near]
    blocks = [block for pair in zip(near, far) for block in pair]
    source = jnp.stack([me ^ b for b in range(holders)]).astype(jnp.int32)

    times = timesteps[0]
    facts = jnp.concatenate([heights[0], widths[0], times >> 5, times & 31]).astype(bf16)
    facts = jnp.tile(jnp.pad(facts, (0, owned - facts.shape[0])), holders)
    extra = jnp.pad(facts[None, :], ((0, 15), (0, 0)))
    cotan = lax.all_to_all(
        jnp.concatenate([cotangent, extra], axis=0).reshape(rows + 16, holders, owned),
        "fsdp",
        1,
        0,
    )
    facts = cotan[:, rows, : 4 * IMAGES].astype(jnp.int32)
    meta = facts[:, : 2 * IMAGES]
    times = facts[:, 2 * IMAGES : 3 * IMAGES] * 32 + facts[:, 3 * IMAGES :]
    embed = timestep_features(times, feature_count)
    embed = jnp.pad(embed, ((0, 0), (0, IMAGES), (0, 0))).reshape(holders * 2 * IMAGES, -1)

    group = jnp.arange(channels) // (channels // GROUPS)
    same = (group[:, None] == group[None, :]).astype(bf16)
    gain = norm_gain[None, :]
    shift = norm_shift[None, :]
    padded = -(-owned // 16) * 16
    low_taps = 4
    time_width = -(-feature_count // LANES) * LANES
    total_rows = holders * rows

    shape = jax.ShapeDtypeStruct
    low, high, act, normed, rstd, taps = call(
        functools.partial(weight_grad_kernel, holders, low_taps),
        (
            shape((owned, low_taps * channels + time_width), bf16),
            shape((owned, (9 - low_taps) * channels), bf16),
            shape((total_rows, channels), bf16),
            shape((holders, rows, channels), f32),
            shape((rows, channels), f32),
            shape((holders, rows, 9 * rows), bf16),
        ),
        [
            pltpu.VMEM((holders * IMAGES, channels), f32),
            pltpu.VMEM((holders, 2 * IMAGES, owned), f32),
            pltpu.VMEM((9 * padded, total_rows), bf16),
        ],
        4 * 9 * padded * total_rows * channels,
        source,
        meta,
        *blocks,
        cotan,
        embed,
        same,
        gain,
        shift,
    )
    block_out, own, other, terms = call(
        functools.partial(conv_kernel, holders),
        (
            shape((holders, rows, owned), bf16),
            shape((chips, rows, channels), bf16),
            shape((chips, rows, channels), bf16),
            shape((8, channels), f32),
        ),
        [
            pltpu.VMEM((9 * LANES, channels), bf16),
            pltpu.VMEM((holders, 2 * IMAGES, owned), f32),
            pltpu.VMEM((total_rows, 9 * LANES), bf16),
            pltpu.VMEM((2 * rows, 9 * LANES), f32),
        ],
        8 * 9 * padded * total_rows * channels,
        source,
        meta,
        act,
        normed,
        taps,
        cotan,
        embed,
        conv_weight,
        time_weight,
        gain,
        shift,
    )

    bits = [1 << i for i in range((replicas - 1).bit_length())]
    sums = []
    for part, order in ((low, bits), (high, bits[::-1])):
        total = part
        for step, bit in enumerate(order):
            total = total.astype(bf16)
            total = total.astype(f32) + exchange(total, "dp", bit).astype(f32)
        sums.append(total * scale)
    grad_conv = jnp.concatenate([sums[0][:, : low_taps * channels], sums[1]], axis=1)
    grad_time = sums[0][:, low_taps * channels : low_taps * channels + feature_count]

    met = exchange(other, "fsdp", 1)
    grad_act = own[0].astype(f32) + met[0].astype(f32)
    for k in range(1, chips):
        part = (own[k].astype(f32) + met[k].astype(f32)).astype(bf16)
        grad_act = grad_act + exchange(part, "fsdp", 2 * k).astype(f32)
    grad_features = call(
        norm_grad_kernel,
        shape((rows, channels), bf16),
        [],
        1 << 20,
        source,
        meta,
        grad_act,
        normed,
        rstd,
        same,
        gain,
        shift,
    )

    returned = lax.all_to_all(block_out, "fsdp", 0, 0)
    block_out = returned.transpose(1, 0, 2).reshape(rows, out_channels)

    for axis, size in (("fsdp", holders), ("dp", replicas)):
        for i in range((size - 1).bit_length()):
            terms = terms + exchange(terms, axis, 1 << i)
    return (block_out, grad_features, grad_conv, grad_time, terms[0] * scale, terms[1] * scale)


def solution(mesh):
    rows = P(("dp", "fsdp"), None)
    owned = P("fsdp", None)
    return jax.shard_map(
        shards,
        mesh=mesh,
        in_specs=(rows, rows, rows, rows, P(), P(), owned, owned, rows),
        out_specs=(rows, rows, owned, owned, P(), P()),
        check_vma=False,
    )
```

```python
import functools
import math

import jax
import jax.numpy as jnp
from jax import lax
from jax.experimental import pallas as pl
from jax.experimental.pallas import tpu as pltpu
from jax.sharding import PartitionSpec as P

GROUPS = 32
IMAGES = 4
LANES = 128

bf16 = jnp.bfloat16
f32 = jnp.float32


def dot(a, b, dims=((1,), (0,))):
    return lax.dot_general(a, b, (dims, ((), ())), preferred_element_type=f32)


def split3(x):
    hi = x.astype(bf16)
    rest = x - hi.astype(f32)
    mid = rest.astype(bf16)
    low = (rest - mid.astype(f32)).astype(bf16)
    return hi, mid, low


def exact_dot(x, ones):
    rows = x.shape[0]
    out = dot(jnp.concatenate(split3(x), axis=0), ones)
    return out[:rows] + out[rows : 2 * rows] + out[2 * rows :]


def bounds_of(heights, widths):
    start = heights[0] * 0
    found = []
    for height, width in zip(heights, widths):
        area = height * width
        found.append((start, start + area, width, area))
        start = start + area
    return found


def inverse_area(area):
    return 1.0 / jnp.maximum(area, 1).astype(f32)


def masks(bounds, shape):
    row = lax.broadcasted_iota(jnp.int32, shape, 0)
    return [(row >= start) & (row < end) for start, end, _, _ in bounds]


def spread(members, table, shape):
    out = jnp.zeros(shape, f32)
    for j in range(IMAGES):
        out = jnp.where(members[j], table[j : j + 1, :], out)
    return out


def image_sums(members, values, bounds):
    sums = []
    for j in range(IMAGES):
        total = jnp.sum(jnp.where(members[j], values, 0.0), axis=0, keepdims=True)
        sums.append(total * inverse_area(bounds[j][3]))
    return jnp.concatenate(sums, axis=0)


def tap_matrices(bounds, rows):
    shape = (rows, rows)
    row = lax.broadcasted_iota(jnp.int32, shape, 0)
    gap = lax.broadcasted_iota(jnp.int32, shape, 1) - row
    width = jnp.zeros(shape, jnp.int32)
    area = jnp.zeros(shape, jnp.int32)
    first = jnp.zeros(shape, jnp.int32)
    for start, end, wide, size in bounds:
        member = (row >= start) & (row < end)
        width = jnp.where(member, wide, width)
        area = jnp.where(member, size, area)
        first = jnp.where(member, start, first)
    offset = row - first
    column = offset & (width - 1)
    columns = {-1: column >= 1, 0: column >= 0, 1: column + 1 < width}
    taps = []
    for shift_row in (-1, 0, 1):
        moved = offset + shift_row * width
        inside = (moved >= 0) & (moved < area)
        left = gap - shift_row * width
        for shift_col in (-1, 0, 1):
            hit = inside & columns[shift_col] & (left == shift_col)
            taps.append(jnp.where(hit, 1.0, 0.0).astype(bf16))
    return taps


def group_matrices(channels):
    size = channels // GROUPS
    channel = lax.broadcasted_iota(jnp.int32, (channels, LANES), 0)
    group = lax.broadcasted_iota(jnp.int32, (channels, LANES), 1)
    down = jnp.where((channel >= group * size) & (channel < (group + 1) * size), 1.0, 0.0)
    channel = lax.broadcasted_iota(jnp.int32, (LANES, channels), 1)
    group = lax.broadcasted_iota(jnp.int32, (LANES, channels), 0)
    back = jnp.where((channel >= group * size) & (channel < (group + 1) * size), 1.0, 0.0)
    return down.astype(bf16), back.astype(bf16)


def group_means(sums, matrices):
    down, back = matrices
    size = down.shape[0] // GROUPS
    return exact_dot(exact_dot(sums, down) * (1.0 / size), back)


def prepare_kernel(
    owned, me_ref, heights_ref, widths_ref, times_ref, features_ref, cotan_ref, *sent
):
    rows, channels = features_ref.shape
    holders = cotan_ref.shape[1] // owned
    padded = -(-owned // 16) * 16
    place = lax.broadcasted_iota(jnp.int32, (16, LANES), 0)
    facts = jnp.zeros((16, LANES), f32)
    for j in range(IMAGES):
        time = times_ref[0, j]
        for i, value in enumerate((heights_ref[0, j], widths_ref[0, j], time >> 5, time & 31)):
            facts = jnp.where(place == i * IMAGES + j, value.astype(f32), facts)
    facts = facts.astype(bf16)
    turned = cotan_ref[...].astype(f32).T
    chip = me_ref[0] >> 1
    slots = []
    for s in range(holders):
        part = turned[s * owned : (s + 1) * owned]
        if padded > owned:
            part = jnp.concatenate([part, jnp.zeros((padded - owned, rows), f32)], axis=0)
        slots.append(part.astype(bf16))
    first = 0
    for ref in sent:
        count = max(first, 1)
        for s in range(holders):
            slot = (chip ^ (s // 2)) - first

            @pl.when((slot >= 0) & (slot < count))
            def _():
                start = pl.multiple_of((2 * slot + s % 2) * padded, 16)
                ref[pl.ds(start, padded), :] = slots[s]

        top = count * 2 * padded
        ref[top : top + 16, :] = facts
        for q in range(channels // LANES):
            start = top + 16 + q * rows
            ref[start : start + rows, :] = features_ref[:, q * LANES : (q + 1) * LANES]
        first = max(2 * first, 1)


def weight_kernel(me_ref, conv_ref, out_ref):
    owned = conv_ref.shape[0]
    channels = out_ref.shape[1]
    padded = -(-owned // 16) * 16
    for t in range(9):
        part = conv_ref[:, t * channels : (t + 1) * channels]
        if padded > owned:
            part = jnp.concatenate([part, jnp.zeros((padded - owned, channels), bf16)], axis=0)
        out_ref[t * LANES : t * LANES + padded, :] = part
        if padded < LANES:
            out_ref[t * LANES + padded : (t + 1) * LANES, :] = jnp.zeros(
                (LANES - padded, channels), bf16
            )


def chunk_sums(members, chunks, inverses):
    out = []
    for chunk in chunks:
        sums = [
            jnp.sum(jnp.where(member, chunk, 0.0), axis=0, keepdims=True) * inverse
            for member, inverse in zip(members, inverses)
        ]
        out.append(jnp.concatenate(sums, axis=0))
    return jnp.concatenate(out, axis=1)


def block_facts(ref, top):
    facts = ref[top : top + 16, :].astype(f32)
    sizes = [facts[j : j + 1, :].astype(jnp.int32) for j in range(2 * IMAGES)]
    times = facts[2 * IMAGES : 3 * IMAGES] * 32.0 + facts[3 * IMAGES :]
    return bounds_of(sizes[:IMAGES], sizes[IMAGES:]), times


def norm_kernel(
    slot,
    top,
    keep,
    features,
    me_ref,
    near_ref,
    far_ref,
    affine_ref,
    turned_ref,
    act_ref,
    sums_ref,
    embed_ref,
    taps_ref,
    slopes_ref,
    norms_ref,
    *kept,
):
    padded = turned_ref.shape[0] // 9
    rows = LANES
    channels = act_ref.shape[1]
    count = channels // LANES
    start = pl.multiple_of((2 * slot + (me_ref[0] & 1)) * padded, 16)
    found = []
    chunks = []
    times = []
    for b, ref in enumerate((near_ref, far_ref)):
        bounds, time = block_facts(ref, top)
        times.append(time)
        taps = jnp.concatenate(tap_matrices(bounds, rows), axis=1)
        taps_ref[b * rows : (b + 1) * rows, :] = taps
        found.append((masks(bounds, (rows, LANES)), [inverse_area(size) for *_, size in bounds]))
        cotan = ref[pl.ds(start, padded), :]
        turned = dot(cotan, taps).astype(bf16)
        for t in range(9):
            turned_ref[t * padded : (t + 1) * padded, b * rows : (b + 1) * rows] = turned[
                :, t * rows : (t + 1) * rows
            ]
        image = lax.broadcasted_iota(jnp.int32, (IMAGES, rows), 0)
        place = lax.broadcasted_iota(jnp.int32, (IMAGES, rows), 1)
        member = jnp.zeros((IMAGES, rows), f32)
        for j in range(IMAGES):
            begin, end, _, _ = bounds[j]
            member = jnp.where((image == j) & (place >= begin) & (place < end), 1.0, member)
        sums_ref[b * IMAGES : (b + 1) * IMAGES, :] = dot(member.astype(bf16), cotan, ((1,), (1,)))
        first = top + 16
        chunks.append(
            [ref[first + q * rows : first + (q + 1) * rows, :].astype(f32) for q in range(count)]
        )

    matrices = group_matrices(channels)
    sums = [chunk_sums(found[b][0], chunks[b], found[b][1]) for b in range(2)]
    means = group_means(jnp.concatenate(sums, axis=0), matrices)
    sums = []
    for b in range(2):
        members, inverses = found[b]
        for q in range(count):
            mean = means[b * IMAGES : (b + 1) * IMAGES, q * LANES : (q + 1) * LANES]
            chunks[b][q] = chunks[b][q] - spread(members, mean, (rows, LANES))
        sums.append(chunk_sums(members, [c * c for c in chunks[b]], inverses))
    rstds = lax.rsqrt(group_means(jnp.concatenate(sums, axis=0), matrices) + 1e-05)
    for b in range(2):
        members = found[b][0]
        for q in range(count):
            here = slice(b * rows, (b + 1) * rows), slice(q * LANES, (q + 1) * LANES)
            rstd = rstds[b * IMAGES : (b + 1) * IMAGES, q * LANES : (q + 1) * LANES]
            rstd = spread(members, rstd, (rows, LANES))
            normed = chunks[b][q] * rstd
            shifted = normed * affine_ref[0:1, here[1]] + affine_ref[1:2, here[1]]
            sig = jax.nn.sigmoid(shifted)
            act_ref[here] = (shifted * sig).astype(bf16)
            slopes_ref[here] = sig * (1.0 + shifted * (1.0 - sig))
            norms_ref[here] = normed
            if keep and b == 0:
                kept[0][:, here[1]] = rstd

    half = features // 2
    place = lax.broadcasted_iota(jnp.int32, (2 * IMAGES, half), 1).astype(f32)
    rates = jnp.exp(-math.log(10000.0) * place / half)
    angles = jnp.concatenate(times, axis=0)[:, :1] * rates
    embed_ref[...] = jnp.concatenate([jnp.sin(angles), jnp.cos(angles)], axis=1)


def conv_kernel(
    slot,
    top,
    owned,
    me_ref,
    near_ref,
    far_ref,
    act_ref,
    embed_ref,
    taps_ref,
    slopes_ref,
    norms_ref,
    weights_ref,
    time_ref,
    before_ref,
    own_ref,
    other_ref,
    terms_ref,
    product,
):
    rows = LANES
    channels = act_ref.shape[1]
    count = channels // LANES
    padded = own_ref.shape[0] - count * rows
    start = pl.multiple_of((2 * slot + (me_ref[0] & 1)) * padded, 16)
    weights = weights_ref[...]
    moved = []
    tiles = []
    for b, ref in enumerate((near_ref, far_ref)):
        taps = taps_ref[b * rows : (b + 1) * rows, :]
        tiles.append(taps)
        cotan = ref[pl.ds(start, padded), :]
        if padded < LANES:
            cotan = jnp.concatenate([cotan, jnp.zeros((LANES - padded, rows), bf16)], axis=0)
        stacked = [taps[:, (8 - t) * rows : (9 - t) * rows] for t in range(9)]
        shifted = dot(jnp.concatenate(stacked, axis=0), cotan, ((1,), (1,))).astype(bf16)
        moved.append(
            jnp.concatenate([shifted[t * rows : (t + 1) * rows] for t in range(9)], axis=1)
        )
    grad_act = dot(jnp.concatenate(moved, axis=0), weights)
    slope = grad_act * slopes_ref[...]
    terms_ref[...] = before_ref[...] + jnp.concatenate(
        [
            jnp.sum(slope * norms_ref[...], axis=0, keepdims=True),
            jnp.sum(slope, axis=0, keepdims=True),
            jnp.zeros((6, channels), f32),
        ],
        axis=0,
    )
    grad_act = grad_act.astype(bf16)
    product[...] = dot(act_ref[...], weights, ((1,), (1,)))
    bias = dot(embed_ref[...].astype(bf16), time_ref[...], ((1,), (1,)))
    if owned < LANES:
        bias = jnp.concatenate([bias, jnp.zeros((2 * IMAGES, LANES - owned), f32)], axis=1)
    for b, (ref, source) in enumerate(((own_ref, near_ref), (other_ref, far_ref))):
        for q in range(count):
            ref[q * rows : (q + 1) * rows, :] = grad_act[
                b * rows : (b + 1) * rows, q * LANES : (q + 1) * LANES
            ]
        values = product[b * rows : (b + 1) * rows, :]
        high = values.astype(bf16)
        low = (values - high.astype(f32)).astype(bf16)
        parts = [high[:, t * LANES : (t + 1) * LANES] for t in range(9)]
        parts += [low[:, t * LANES : (t + 1) * LANES] for t in range(9)]
        total = dot(
            jnp.concatenate([tiles[b], tiles[b]], axis=1), jnp.concatenate(parts, axis=0)
        )
        members = masks(block_facts(source, top)[0], (rows, LANES))
        total = total + spread(members, bias[b * IMAGES : (b + 1) * IMAGES], (rows, LANES))
        ref[count * rows :, :] = total.T[:padded].astype(bf16)


def weight_grad_kernel(pairs, low_taps, owned, *refs):
    turned, act, sums, embed = (
        [ref[...] for ref in refs[i * pairs : (i + 1) * pairs]] for i in range(4)
    )
    low_ref, high_ref = refs[4 * pairs :]
    channels = act[0].shape[1]
    padded = turned[0].shape[0] // 9
    grad = dot(jnp.concatenate(turned, axis=1), jnp.concatenate(act, axis=0))
    for t in range(9):
        part = grad[t * padded : t * padded + owned].astype(bf16)
        if t < low_taps:
            low_ref[:, t * channels : (t + 1) * channels] = part
        else:
            high_ref[:, (t - low_taps) * channels : (t - low_taps + 1) * channels] = part
    embed = jnp.concatenate(embed, axis=0).astype(bf16)
    time_grad = jnp.zeros((padded, embed.shape[1]), f32)
    for term in split3(jnp.concatenate(sums, axis=0)):
        time_grad = time_grad + dot(term, embed, ((0,), (0,)))
    spare = low_ref.shape[1] - low_taps * channels - embed.shape[1]
    low_ref[:, low_taps * channels :] = jnp.concatenate(
        [time_grad[:owned], jnp.zeros((owned, spare), f32)], axis=1
    ).astype(bf16)


def join_kernel(owned, own_ref, met_ref, out_ref):
    size = own_ref.shape[0]
    padded = -(-owned // 16) * 16
    top = size - padded
    total = own_ref[:top, :].astype(f32) + met_ref[:top, :].astype(f32)
    out_ref[:top, :] = total.astype(out_ref.dtype)
    out_ref[top:size, :] = own_ref[top:, :].astype(out_ref.dtype)
    out_ref[size:, :] = met_ref[top:, :].astype(out_ref.dtype)


def norm_grad_kernel(
    owned,
    chips,
    me_ref,
    heights_ref,
    widths_ref,
    *refs,
):
    terms = refs[:chips]
    normed_ref, rstd_ref, affine_ref, out_ref, grad_ref, joined = refs[chips:]
    rows, channels = rstd_ref.shape
    top = channels // LANES * rows
    padded = (terms[0].shape[0] - top) // 2
    me = me_ref[0]
    pieces = []
    for ref in terms:
        pieces += [ref[top : top + padded, :], ref[top + padded :, :]]
    for b, piece in enumerate(pieces):
        start = pl.multiple_of((me ^ b) * owned, 8)
        joined[pl.ds(start, owned), :] = piece[:owned].astype(f32)
    out_ref[...] = joined[...].T.astype(bf16)

    total = terms[0][:top, :]
    for ref in terms[1:]:
        total = total + ref[:top, :].astype(f32)
    total = jnp.concatenate(
        [total[q * rows : (q + 1) * rows] for q in range(channels // LANES)], axis=1
    )
    normed = normed_ref[:rows, :]
    gain = affine_ref[0:1, :]
    shifted = normed * gain + affine_ref[1:2, :]
    sig = jax.nn.sigmoid(shifted)
    slope = total * (sig * (1.0 + shifted * (1.0 - sig)))
    grad = slope * gain
    bounds = bounds_of(
        [heights_ref[0, j] for j in range(IMAGES)], [widths_ref[0, j] for j in range(IMAGES)]
    )
    members = masks(bounds, (rows, channels))
    sums = jnp.concatenate(
        [image_sums(members, grad, bounds), image_sums(members, grad * normed, bounds)], axis=0
    )
    means = group_means(sums, group_matrices(channels))
    mean_grad = spread(members, means[:IMAGES], (rows, channels))
    mean_cross = spread(members, means[IMAGES:], (rows, channels))
    grad_ref[...] = (rstd_ref[...] * (grad - mean_grad - normed * mean_cross)).astype(bf16)


def finish_kernel(scale, low_ref, low_met_ref, high_ref, high_met_ref, conv_ref, time_ref):
    low = (low_ref[...].astype(f32) + low_met_ref[...].astype(f32)) * scale
    width = conv_ref.shape[1] - high_ref.shape[1]
    conv_ref[:, :width] = low[:, :width]
    time_ref[...] = low[:, width : width + time_ref.shape[1]]
    conv_ref[:, width:] = (high_ref[...].astype(f32) + high_met_ref[...].astype(f32)) * scale


def call(kernel, outs, scratch, limit, scalars, microseconds, *args):
    smem = pl.BlockSpec(memory_space=pltpu.SMEM)
    vmem = pl.BlockSpec(memory_space=pltpu.VMEM)
    return pl.pallas_call(
        kernel,
        out_shape=outs,
        in_specs=[smem] * scalars + [vmem] * (len(args) - scalars),
        out_specs=jax.tree.map(lambda _: vmem, outs),
        scratch_shapes=scratch,
        compiler_params=pltpu.CompilerParams(vmem_limit_bytes=limit << 20),
        cost_estimate=pl.CostEstimate(
            flops=int(microseconds * 0.01 * 1e9),
            bytes_accessed=int(microseconds * 0.01 * 3e6),
            transcendentals=0,
        ),
    )(*args)


def exchange(value, axis, bit):
    size = lax.axis_size(axis)
    return lax.ppermute(value, axis, [(i, i ^ bit) for i in range(size)])


def together(*values):
    return lax.optimization_barrier(values)


def shards(
    features, heights, widths, timesteps, norm_gain, norm_shift, conv_weight, time_weight, cotangent
):
    rows, channels = features.shape
    replicas = lax.axis_size("dp")
    holders = lax.axis_size("fsdp")
    chips = holders // 2
    owned = conv_weight.shape[0]
    out_channels = cotangent.shape[1]
    feature_count = time_weight.shape[1]
    scale = 1.0 / math.sqrt(replicas * holders * rows)
    me = lax.axis_index("fsdp").astype(jnp.int32)[None]
    padded = -(-owned // 16) * 16
    low_taps = 4
    time_width = -(-feature_count // LANES) * LANES
    shape = jax.ShapeDtypeStruct
    affine = jnp.stack([norm_gain, norm_shift])

    roots = [0] + [1 << i for i in range((chips - 1).bit_length())]
    tops = [2 * padded * max(root, 1) for root in roots]
    sent = call(
        functools.partial(prepare_kernel, owned),
        [shape((top + 16 + channels // LANES * rows, LANES), bf16) for top in tops],
        [],
        60,
        4,
        2.0,
        me,
        heights,
        widths,
        timesteps,
        features,
        cotangent,
    )
    returned = channels // LANES * rows + padded
    near, far, normed, results = [sent[0]], [], [], {}
    terms = jnp.zeros((8, channels), f32)

    def slot_and_top(k):
        return k - roots[k.bit_length()], tops[k.bit_length()]

    def convolve(k, me, weights, terms):
        return call(
            functools.partial(conv_kernel, *slot_and_top(k), owned),
            (
                shape((returned, LANES), bf16),
                shape((returned, LANES), bf16),
                shape((8, channels), f32),
            ),
            [pltpu.VMEM((2 * rows, 9 * LANES), f32)],
            16,
            1,
            2.0,
            me,
            near[k],
            far[k],
            normed[k][1],
            *normed[k][3:7],
            weights,
            time_weight,
            terms,
        )

    def join(k, dtype):
        own, other = results[k]
        return call(
            functools.partial(join_kernel, owned),
            shape((returned + padded, LANES), dtype),
            [],
            8,
            0,
            0.1,
            own,
            exchange(other, "fsdp", 1),
        )

    here = me
    for k in range(chips):
        low_bit = k & -k
        if k:
            from_here = sent[k.bit_length()] if k == low_bit else near[k - low_bit]
            near.append(exchange(from_here, "fsdp", 2 * low_bit))
            if k > 1:
                near[k], normed[-1][2], terms = together(near[k], normed[-1][2], terms)
            if k == chips - 1 and k > 1:
                *results[k - 1], terms = convolve(k - 1, here, weights, terms)
            near[k], here, terms = together(near[k], here, terms)
            if k - 1 not in results:
                *results[k - 1], terms = convolve(k - 1, here, weights, terms)
        far.append(exchange(near[k], "fsdp", 1))
        normed.append(
            call(
                functools.partial(norm_kernel, *slot_and_top(k), k == 0, feature_count),
                [
                    shape((9 * padded, 2 * rows), bf16),
                    shape((2 * rows, channels), bf16),
                    shape((2 * IMAGES, padded), f32),
                    shape((2 * IMAGES, feature_count), f32),
                    shape((2 * rows, 9 * rows), bf16),
                    shape((2 * rows, channels), f32),
                    shape((2 * rows, channels), f32),
                ]
                + [shape((rows, channels), f32)] * (k == 0),
                [],
                16,
                1,
                2.0,
                me,
                near[k],
                far[k],
                affine,
            )
        )
        normed[-1] = list(normed[-1])
        if k == 0:
            normed[0][2], here = together(normed[0][2], me)
            weights = call(
                weight_kernel,
                shape((9 * LANES, channels), bf16),
                [],
                16,
                1,
                2.0,
                here,
                conv_weight,
            )
            *results[0], terms = convolve(0, here, weights, terms)
    rstd = normed[0][7]
    joined = [join(k, bf16 if k else f32) for k in range(chips - 1)]
    normed[-1][2], *joined = together(normed[-1][2], *joined)
    low, high = call(
        functools.partial(weight_grad_kernel, chips, low_taps, owned),
        (
            shape((owned, low_taps * channels + time_width), bf16),
            shape((owned, (9 - low_taps) * channels), bf16),
        ),
        [],
        min(60, 6 * chips),
        0,
        1.5,
        *(result[i] for i in range(4) for result in normed),
    )

    bits = [1 << i for i in range((replicas - 1).bit_length())]
    low, high, here = together(low, high, here)
    totals = [low, high]
    received = [exchange(t, "dp", bit) for t, bit in zip(totals, (bits[0], bits[-1]))]

    grads = [joined[0]] + [exchange(joined[k], "fsdp", 2 * k) for k in range(1, chips - 1)]
    last = chips - 1
    *results[last], terms = convolve(last, here, weights, terms)
    part, *grads[1:] = together(join(last, bf16), *grads[1:])
    grads.append(exchange(part, "fsdp", 2 * last))
    for i in range((holders - 1).bit_length()):
        if i == 1:
            received, terms, grads[1:last] = together(received, terms, grads[1:last])
        terms = terms + exchange(terms, "fsdp", 1 << i)

    for step in range(1, len(bits)):
        totals = [
            (t.astype(f32) + r.astype(f32)).astype(bf16) for t, r in zip(totals, received)
        ]
        orders = (bits[step], bits[-1 - step])
        received = [exchange(t, "dp", bit) for t, bit in zip(totals, orders)]
    totals, grads[0], terms = lax.optimization_barrier((totals, grads[0], terms))
    grad_conv, grad_time = call(
        functools.partial(finish_kernel, scale),
        (shape((owned, 9 * channels), f32), shape((owned, feature_count), f32)),
        [],
        16,
        0,
        1.5,
        totals[0],
        received[0],
        totals[1],
        received[1],
    )
    block_out, grad_features = call(
        functools.partial(norm_grad_kernel, owned, chips),
        (shape((rows, out_channels), bf16), shape((rows, channels), bf16)),
        [pltpu.VMEM((out_channels, rows), f32)],
        16,
        3,
        2.5,
        me,
        heights,
        widths,
        *grads,
        normed[0][6],
        rstd,
        affine,
    )
    for bit in bits:
        terms = terms + exchange(terms, "dp", bit)
    return (block_out, grad_features, grad_conv, grad_time, terms[0] * scale, terms[1] * scale)


def solution(mesh):
    rows = P(("dp", "fsdp"), None)
    owned = P("fsdp", None)
    return jax.shard_map(
        shards,
        mesh=mesh,
        in_specs=(rows, rows, rows, rows, P(), P(), owned, owned, rows),
        out_specs=(rows, rows, owned, owned, P(), P()),
        check_vma=False,
    )
```

```python
import functools
import math

import jax
import jax.numpy as jnp
from jax import lax
from jax.experimental import pallas as pl
from jax.experimental.pallas import tpu as pltpu
from jax.sharding import PartitionSpec as P

GROUPS = 32
IMAGES = 4
LANES = 128
TERM_ROWS = 32

bf16 = jnp.bfloat16
f32 = jnp.float32


def dot(a, b, dims=((1,), (0,))):
    return lax.dot_general(a, b, (dims, ((), ())), preferred_element_type=f32)


def split3(x):
    hi = x.astype(bf16)
    rest = x - hi.astype(f32)
    mid = rest.astype(bf16)
    low = (rest - mid.astype(f32)).astype(bf16)
    return hi, mid, low


def exact_dot(x, ones):
    rows = x.shape[0]
    out = dot(jnp.concatenate(split3(x), axis=0), ones)
    return out[:rows] + out[rows : 2 * rows] + out[2 * rows :]


def bounds_of(heights, widths):
    start = heights[0] * 0
    found = []
    for height, width in zip(heights, widths):
        area = height * width
        found.append((start, start + area, width, area))
        start = start + area
    return found


def inverse_area(area):
    return 1.0 / jnp.maximum(area, 1).astype(f32)


def masks(bounds, shape):
    row = lax.broadcasted_iota(jnp.int32, shape, 0)
    return [(row >= start) & (row < end) for start, end, _, _ in bounds]


def spread(members, table, shape):
    out = jnp.zeros(shape, f32)
    for j in range(IMAGES):
        out = jnp.where(members[j], table[j : j + 1, :], out)
    return out


def image_sums(members, values, bounds):
    sums = []
    for j in range(IMAGES):
        total = jnp.sum(jnp.where(members[j], values, 0.0), axis=0, keepdims=True)
        sums.append(total * inverse_area(bounds[j][3]))
    return jnp.concatenate(sums, axis=0)


def tap_matrices(bounds, rows):
    shape = (rows, rows)
    row = lax.broadcasted_iota(jnp.int32, shape, 0)
    gap = lax.broadcasted_iota(jnp.int32, shape, 1) - row
    width = jnp.zeros(shape, jnp.int32)
    area = jnp.zeros(shape, jnp.int32)
    first = jnp.zeros(shape, jnp.int32)
    for start, end, wide, size in bounds:
        member = (row >= start) & (row < end)
        width = jnp.where(member, wide, width)
        area = jnp.where(member, size, area)
        first = jnp.where(member, start, first)
    offset = row - first
    column = offset & (width - 1)
    columns = {-1: column >= 1, 0: column >= 0, 1: column + 1 < width}
    taps = []
    for shift_row in (-1, 0, 1):
        moved = offset + shift_row * width
        inside = (moved >= 0) & (moved < area)
        left = gap - shift_row * width
        for shift_col in (-1, 0, 1):
            hit = inside & columns[shift_col] & (left == shift_col)
            taps.append(jnp.where(hit, 1.0, 0.0).astype(bf16))
    return taps


def group_matrices(channels):
    size = channels // GROUPS
    channel = lax.broadcasted_iota(jnp.int32, (channels, LANES), 0)
    group = lax.broadcasted_iota(jnp.int32, (channels, LANES), 1)
    down = jnp.where((channel >= group * size) & (channel < (group + 1) * size), 1.0, 0.0)
    channel = lax.broadcasted_iota(jnp.int32, (LANES, channels), 1)
    group = lax.broadcasted_iota(jnp.int32, (LANES, channels), 0)
    back = jnp.where((channel >= group * size) & (channel < (group + 1) * size), 1.0, 0.0)
    return down.astype(bf16), back.astype(bf16)


def group_means(sums, matrices):
    down, back = matrices
    size = down.shape[0] // GROUPS
    return exact_dot(exact_dot(sums, down) * (1.0 / size), back)


def prepare_kernel(
    owned, me_ref, heights_ref, widths_ref, times_ref, features_ref, cotan_ref, *sent
):
    rows, channels = features_ref.shape
    holders = cotan_ref.shape[1] // owned
    padded = -(-owned // 16) * 16
    place = lax.broadcasted_iota(jnp.int32, (16, LANES), 0)
    facts = jnp.zeros((16, LANES), f32)
    for j in range(IMAGES):
        time = times_ref[0, j]
        for i, value in enumerate((heights_ref[0, j], widths_ref[0, j], time >> 5, time & 31)):
            facts = jnp.where(place == i * IMAGES + j, value.astype(f32), facts)
    facts = facts.astype(bf16)
    turned = cotan_ref[...].astype(f32).T
    chip = me_ref[0] >> 1
    slots = []
    for s in range(holders):
        part = turned[s * owned : (s + 1) * owned]
        if padded > owned:
            part = jnp.concatenate([part, jnp.zeros((padded - owned, rows), f32)], axis=0)
        slots.append(part.astype(bf16))
    first = 0
    for ref in sent:
        count = max(first, 1)
        for s in range(holders):
            slot = (chip ^ (s // 2)) - first

            @pl.when((slot >= 0) & (slot < count))
            def _():
                start = pl.multiple_of((2 * slot + s % 2) * padded, 16)
                ref[pl.ds(start, padded), :] = slots[s]

        top = count * 2 * padded
        ref[top : top + 16, :] = facts
        for q in range(channels // LANES):
            start = top + 16 + q * rows
            ref[start : start + rows, :] = features_ref[:, q * LANES : (q + 1) * LANES]
        first = max(2 * first, 1)


def chunk_sums(members, chunks, inverses):
    out = []
    for chunk in chunks:
        sums = [
            jnp.sum(jnp.where(member, chunk, 0.0), axis=0, keepdims=True) * inverse
            for member, inverse in zip(members, inverses)
        ]
        out.append(jnp.concatenate(sums, axis=0))
    return jnp.concatenate(out, axis=1)


def block_facts(ref, top):
    facts = ref[top : top + 16, :].astype(f32)
    sizes = [facts[j : j + 1, :].astype(jnp.int32) for j in range(2 * IMAGES)]
    times = facts[2 * IMAGES : 3 * IMAGES] * 32.0 + facts[3 * IMAGES :]
    return bounds_of(sizes[:IMAGES], sizes[IMAGES:]), times


def first_kernel(slot, top, owned, me_ref, near_ref, far_ref, gain_ref, shift_ref, *refs):
    conv_ref, time_ref, own_ref, other_ref, terms_ref, turned_ref, act_ref, sums_ref, embed_ref = refs[:9]
    normed_ref, rstd_ref, weights_ref, held_ref, taps, slopes, norms, product, copied = refs[9:]
    padded = conv_ref.shape[0]
    width = weights_ref.shape[1]
    copies = [pltpu.make_async_copy(time_ref, held_ref, copied.at[9])]
    for t in range(9):
        copies.append(
            pltpu.make_async_copy(
                conv_ref.at[:, pl.ds(t * width, width)],
                weights_ref.at[pl.ds(t * LANES, padded), :],
                copied.at[t],
            )
        )
        if padded < LANES:
            weights_ref[t * LANES + padded : (t + 1) * LANES, :] = jnp.zeros(
                (LANES - padded, width), bf16
            )
    for copy in copies:
        copy.start()
    blocks = me_ref, near_ref, far_ref
    norm_part(
        slot, top, time_ref.shape[1], *blocks, gain_ref, shift_ref, turned_ref, act_ref, sums_ref,
        embed_ref, taps, slopes, norms, rstd_ref,
    )
    normed_ref[...] = norms[: normed_ref.shape[0], :]
    for copy in copies:
        copy.wait()
    conv_part(
        slot, top, owned, *blocks, act_ref, embed_ref, taps, slopes, norms, weights_ref, held_ref,
        None, own_ref, other_ref, terms_ref, product,
    )


def pair_kernel(
    slot,
    top,
    owned,
    me_ref,
    near_ref,
    far_ref,
    gain_ref,
    shift_ref,
    weights_ref,
    time_ref,
    before_ref,
    own_ref,
    other_ref,
    terms_ref,
    turned_ref,
    act_ref,
    sums_ref,
    embed_ref,
    taps,
    slopes,
    norms,
    product,
):
    blocks = me_ref, near_ref, far_ref
    norm_part(
        slot, top, time_ref.shape[1], *blocks, gain_ref, shift_ref, turned_ref, act_ref, sums_ref,
        embed_ref, taps, slopes, norms, None,
    )
    conv_part(
        slot, top, owned, *blocks, act_ref, embed_ref, taps, slopes, norms, weights_ref, time_ref,
        before_ref, own_ref, other_ref, terms_ref, product,
    )


def norm_part(
    slot,
    top,
    features,
    me_ref,
    near_ref,
    far_ref,
    gain_ref,
    shift_ref,
    turned_ref,
    act_ref,
    sums_ref,
    embed_ref,
    taps_ref,
    slopes_ref,
    norms_ref,
    rstd_ref,
):
    gain = gain_ref[...].reshape(1, -1)
    shift = shift_ref[...].reshape(1, -1)
    padded = turned_ref.shape[0] // 9
    rows = LANES
    channels = act_ref.shape[1]
    count = channels // LANES
    start = pl.multiple_of((2 * slot + (me_ref[0] & 1)) * padded, 16)
    found = []
    chunks = []
    times = []
    for b, ref in enumerate((near_ref, far_ref)):
        bounds, time = block_facts(ref, top)
        times.append(time)
        taps = jnp.concatenate(tap_matrices(bounds, rows), axis=1)
        taps_ref[b * rows : (b + 1) * rows, :] = taps
        found.append((masks(bounds, (rows, LANES)), [inverse_area(size) for *_, size in bounds]))
        cotan = ref[pl.ds(start, padded), :]
        turned = dot(cotan, taps).astype(bf16)
        for t in range(9):
            turned_ref[t * padded : (t + 1) * padded, b * rows : (b + 1) * rows] = turned[
                :, t * rows : (t + 1) * rows
            ]
        image = lax.broadcasted_iota(jnp.int32, (IMAGES, rows), 0)
        place = lax.broadcasted_iota(jnp.int32, (IMAGES, rows), 1)
        member = jnp.zeros((IMAGES, rows), f32)
        for j in range(IMAGES):
            begin, end, _, _ = bounds[j]
            member = jnp.where((image == j) & (place >= begin) & (place < end), 1.0, member)
        sums_ref[b * IMAGES : (b + 1) * IMAGES, :] = dot(member.astype(bf16), cotan, ((1,), (1,)))
        first = top + 16
        chunks.append(
            [ref[first + q * rows : first + (q + 1) * rows, :].astype(f32) for q in range(count)]
        )

    matrices = group_matrices(channels)
    sums = [chunk_sums(found[b][0], chunks[b], found[b][1]) for b in range(2)]
    means = group_means(jnp.concatenate(sums, axis=0), matrices)
    sums = []
    for b in range(2):
        members, inverses = found[b]
        for q in range(count):
            mean = means[b * IMAGES : (b + 1) * IMAGES, q * LANES : (q + 1) * LANES]
            chunks[b][q] = chunks[b][q] - spread(members, mean, (rows, LANES))
        sums.append(chunk_sums(members, [c * c for c in chunks[b]], inverses))
    rstds = lax.rsqrt(group_means(jnp.concatenate(sums, axis=0), matrices) + 1e-05)
    for b in range(2):
        members = found[b][0]
        for q in range(count):
            here = slice(b * rows, (b + 1) * rows), slice(q * LANES, (q + 1) * LANES)
            rstd = rstds[b * IMAGES : (b + 1) * IMAGES, q * LANES : (q + 1) * LANES]
            rstd = spread(members, rstd, (rows, LANES))
            normed = chunks[b][q] * rstd
            shifted = normed * gain[:, here[1]] + shift[:, here[1]]
            sig = jax.nn.sigmoid(shifted)
            act_ref[here] = (shifted * sig).astype(bf16)
            slopes_ref[here] = sig * (1.0 + shifted * (1.0 - sig))
            norms_ref[here] = normed
            if rstd_ref is not None and b == 0:
                rstd_ref[:, here[1]] = rstd

    half = features // 2
    place = lax.broadcasted_iota(jnp.int32, (2 * IMAGES, half), 1).astype(f32)
    rates = jnp.exp(-math.log(10000.0) * place / half)
    angles = jnp.concatenate(times, axis=0)[:, :1] * rates
    embed_ref[...] = jnp.concatenate([jnp.sin(angles), jnp.cos(angles)], axis=1)


def conv_part(
    slot,
    top,
    owned,
    me_ref,
    near_ref,
    far_ref,
    act_ref,
    embed_ref,
    taps_ref,
    slopes_ref,
    norms_ref,
    weights_ref,
    time_ref,
    before_ref,
    own_ref,
    other_ref,
    terms_ref,
    product,
):
    rows = LANES
    channels = act_ref.shape[1]
    count = channels // LANES
    padded = own_ref.shape[0] - count * rows
    start = pl.multiple_of((2 * slot + (me_ref[0] & 1)) * padded, 16)
    weights = weights_ref[...]
    moved = []
    tiles = []
    for b, ref in enumerate((near_ref, far_ref)):
        taps = taps_ref[b * rows : (b + 1) * rows, :]
        tiles.append(taps)
        cotan = ref[pl.ds(start, padded), :]
        if padded < LANES:
            cotan = jnp.concatenate([cotan, jnp.zeros((LANES - padded, rows), bf16)], axis=0)
        stacked = [taps[:, (8 - t) * rows : (9 - t) * rows] for t in range(9)]
        shifted = dot(jnp.concatenate(stacked, axis=0), cotan, ((1,), (1,))).astype(bf16)
        moved.append(
            jnp.concatenate([shifted[t * rows : (t + 1) * rows] for t in range(9)], axis=1)
        )
    grad_act = dot(jnp.concatenate(moved, axis=0), weights)
    slope = grad_act * slopes_ref[...]
    terms = jnp.concatenate(
        [
            jnp.sum(slope * norms_ref[...], axis=0, keepdims=True),
            jnp.sum(slope, axis=0, keepdims=True),
            jnp.zeros((6, channels), f32),
        ],
        axis=0,
    )
    if before_ref is not None:
        terms = terms + before_ref[...]
    terms_ref[...] = terms
    other_ref[count * rows + padded :, :] = term_rows(terms)
    grad_act = grad_act.astype(bf16)
    product[...] = dot(act_ref[...], weights, ((1,), (1,)))
    bias = dot(embed_ref[...].astype(bf16), time_ref[...], ((1,), (1,)))
    if owned < LANES:
        bias = jnp.concatenate([bias, jnp.zeros((2 * IMAGES, LANES - owned), f32)], axis=1)
    for b, (ref, source) in enumerate(((own_ref, near_ref), (other_ref, far_ref))):
        for q in range(count):
            ref[q * rows : (q + 1) * rows, :] = grad_act[
                b * rows : (b + 1) * rows, q * LANES : (q + 1) * LANES
            ]
        values = product[b * rows : (b + 1) * rows, :]
        high = values.astype(bf16)
        low = (values - high.astype(f32)).astype(bf16)
        parts = [high[:, t * LANES : (t + 1) * LANES] for t in range(9)]
        parts += [low[:, t * LANES : (t + 1) * LANES] for t in range(9)]
        total = dot(
            jnp.concatenate([tiles[b], tiles[b]], axis=1), jnp.concatenate(parts, axis=0)
        )
        members = masks(block_facts(source, top)[0], (rows, LANES))
        total = total + spread(members, bias[b * IMAGES : (b + 1) * IMAGES], (rows, LANES))
        ref[count * rows : count * rows + padded, :] = total.T[:padded].astype(bf16)


def term_rows(terms):
    count = terms.shape[1] // LANES
    parts = [terms[r : r + 1, q * LANES : (q + 1) * LANES] for r in range(2) for q in range(count)]
    whole = jnp.concatenate(parts, axis=0)
    high = whole.astype(bf16).astype(f32)
    rest = jnp.zeros((TERM_ROWS - 4 * count, LANES), f32)
    return jnp.concatenate([high, whole - high, rest], axis=0).astype(bf16)


def terms_of(rows, channels):
    count = channels // LANES
    rows = rows.astype(f32)
    whole = rows[: 2 * count] + rows[2 * count : 4 * count]
    return jnp.concatenate(
        [
            jnp.concatenate([whole[r * count + q : r * count + q + 1] for q in range(count)], axis=1)
            for r in range(2)
        ],
        axis=0,
    )


def weight_grad_kernel(pairs, low_taps, owned, *refs):
    turned, act, sums, embed = (
        [ref[...] for ref in refs[i * pairs : (i + 1) * pairs]] for i in range(4)
    )
    outs = refs[4 * pairs :]

    def put(part, columns, values):
        outs[part][:, columns] = values[:owned].astype(bf16)

    channels = act[0].shape[1]
    padded = turned[0].shape[0] // 9
    grad = dot(jnp.concatenate(turned, axis=1), jnp.concatenate(act, axis=0))
    for t in range(9):
        part, place = (0, t) if t < low_taps else (1, t - low_taps)
        columns = slice(place * channels, (place + 1) * channels)
        put(part, columns, grad[t * padded : (t + 1) * padded])
    embed = jnp.concatenate(embed, axis=0).astype(bf16)
    time_grad = jnp.zeros((padded, embed.shape[1]), f32)
    for term in split3(jnp.concatenate(sums, axis=0)):
        time_grad = time_grad + dot(term, embed, ((0,), (0,)))
    width = outs[0].shape[1]
    spare = width - low_taps * channels - embed.shape[1]
    time_grad = jnp.concatenate([time_grad, jnp.zeros((padded, spare), f32)], axis=1)
    put(0, slice(low_taps * channels, width), time_grad)


def join_kernel(own_ref, met_ref, out_ref):
    size = own_ref.shape[0]
    top = 2 * size - out_ref.shape[0]
    total = own_ref[:top, :].astype(f32) + met_ref[:top, :].astype(f32)
    out_ref[:top, :] = total.astype(out_ref.dtype)
    out_ref[top:size, :] = own_ref[top:, :].astype(out_ref.dtype)
    out_ref[size:, :] = met_ref[top:size, :].astype(out_ref.dtype)


def join_last_kernel(own_ref, met_ref, terms_ref, out_ref, sums_ref):
    join_kernel(own_ref, met_ref, out_ref.at[: out_ref.shape[0] - TERM_ROWS, :])
    channels = terms_ref.shape[1]
    mine = terms_of(term_rows(terms_ref[...]), channels)
    terms = term_rows(mine + terms_of(met_ref[-TERM_ROWS:, :], channels))
    out_ref[out_ref.shape[0] - TERM_ROWS :, :] = terms
    sums_ref[...] = terms


def add_terms_kernel(terms_ref, met_ref, out_ref):
    channels = out_ref.shape[1]
    total = terms_of(terms_ref[...], channels) + terms_of(met_ref[-TERM_ROWS:, :], channels)
    out_ref[...] = jnp.concatenate([total, jnp.zeros((6, channels), f32)], axis=0)


def norm_grad_kernel(
    owned,
    chips,
    me_ref,
    heights_ref,
    widths_ref,
    *refs,
):
    terms = refs[:chips]
    normed_ref, rstd_ref, gain_ref, shift_ref, out_ref, grad_ref, joined = refs[chips:]
    rows, channels = rstd_ref.shape
    top = channels // LANES * rows
    padded = (terms[0].shape[0] - top) // 2
    end = top + 2 * padded
    me = me_ref[0]
    pieces = []
    for ref in terms:
        pieces += [ref[top : top + padded, :], ref[top + padded : end, :]]
    for b, piece in enumerate(pieces):
        start = pl.multiple_of((me ^ b) * owned, 8)
        joined[pl.ds(start, owned), :] = piece[:owned].astype(f32)
    out_ref[...] = joined[...].T.astype(bf16)

    total = terms[0][:top, :]
    for ref in terms[1:]:
        total = total + ref[:top, :].astype(f32)
    total = jnp.concatenate(
        [total[q * rows : (q + 1) * rows] for q in range(channels // LANES)], axis=1
    )
    normed = normed_ref[...]
    gain = gain_ref[...].reshape(1, -1)
    shifted = normed * gain + shift_ref[...].reshape(1, -1)
    sig = jax.nn.sigmoid(shifted)
    slope = total * (sig * (1.0 + shifted * (1.0 - sig)))
    grad = slope * gain
    bounds = bounds_of(
        [heights_ref[0, j] for j in range(IMAGES)], [widths_ref[0, j] for j in range(IMAGES)]
    )
    members = masks(bounds, (rows, channels))
    sums = jnp.concatenate(
        [image_sums(members, grad, bounds), image_sums(members, grad * normed, bounds)], axis=0
    )
    means = group_means(sums, group_matrices(channels))
    mean_grad = spread(members, means[:IMAGES], (rows, channels))
    mean_cross = spread(members, means[IMAGES:], (rows, channels))
    grad_ref[...] = (rstd_ref[...] * (grad - mean_grad - normed * mean_cross)).astype(bf16)


def finish_kernel(scale, low_ref, low_met_ref, high_ref, high_met_ref, conv_ref, time_ref):
    low = (low_ref[...].astype(f32) + low_met_ref[...].astype(f32)) * scale
    width = conv_ref.shape[1] - high_ref.shape[1]
    conv_ref[:, :width] = low[:, :width]
    time_ref[...] = low[:, width : width + time_ref.shape[1]]
    conv_ref[:, width:] = (high_ref[...].astype(f32) + high_met_ref[...].astype(f32)) * scale


def call(kernel, outs, scratch, limit, scalars, microseconds, *args, left=()):
    smem = pl.BlockSpec(memory_space=pltpu.SMEM)
    vmem = pl.BlockSpec(memory_space=pltpu.VMEM)
    return pl.pallas_call(
        kernel,
        out_shape=outs,
        in_specs=[smem] * scalars
        + [vmem] * (len(args) - scalars)
        + [pl.BlockSpec(memory_space=pl.ANY)] * len(left),
        out_specs=jax.tree.map(lambda _: vmem, outs),
        scratch_shapes=scratch,
        compiler_params=pltpu.CompilerParams(vmem_limit_bytes=limit << 20),
        cost_estimate=pl.CostEstimate(
            flops=int(microseconds * 0.5 * 1e9),
            bytes_accessed=int(microseconds * 0.5 * 3e6),
            transcendentals=0,
        ),
    )(*args, *left)


def exchange(value, axis, bit):
    size = lax.axis_size(axis)
    return lax.ppermute(value, axis, [(i, i ^ bit) for i in range(size)])


def together(*values):
    return lax.optimization_barrier(values)


def shards(
    features, heights, widths, timesteps, norm_gain, norm_shift, conv_weight, time_weight, cotangent
):
    rows, channels = features.shape
    replicas = lax.axis_size("dp")
    holders = lax.axis_size("fsdp")
    chips = holders // 2
    owned = conv_weight.shape[0]
    out_channels = cotangent.shape[1]
    feature_count = time_weight.shape[1]
    scale = 1.0 / math.sqrt(replicas * holders * rows)
    me = lax.axis_index("fsdp").astype(jnp.int32)[None]
    padded = -(-owned // 16) * 16
    low_taps = 4
    time_width = -(-feature_count // LANES) * LANES
    shape = jax.ShapeDtypeStruct

    roots = [0] + [1 << i for i in range((chips - 1).bit_length())]
    tops = [2 * padded * max(root, 1) for root in roots]
    sent = call(
        functools.partial(prepare_kernel, owned),
        [shape((top + 16 + channels // LANES * rows, LANES), bf16) for top in tops],
        [],
        60,
        4,
        4.0,
        me,
        heights,
        widths,
        timesteps,
        features,
        cotangent,
    )
    returned = channels // LANES * rows + padded
    last = chips - 1
    if padded > owned:
        conv_rows = jnp.pad(conv_weight, ((0, padded - owned), (0, 0)))
    else:
        conv_rows = conv_weight
    own_shapes = [
        shape((returned, LANES), bf16),
        shape((returned + TERM_ROWS, LANES), bf16),
        shape((8, channels), f32),
    ]
    norm_shapes = [
        shape((9 * padded, 2 * rows), bf16),
        shape((2 * rows, channels), bf16),
        shape((2 * IMAGES, padded), f32),
        shape((2 * IMAGES, feature_count), f32),
    ]
    held = [
        ((2 * rows, 9 * rows), bf16),
        ((2 * rows, channels), f32),
        ((2 * rows, channels), f32),
    ]
    product = pltpu.VMEM((2 * rows, 9 * LANES), f32)

    near, far, ours, normed = [sent[0]], [], [], []
    here = me

    def arrive(k):
        low_bit = k & -k
        from_here = sent[k.bit_length()] if k == low_bit else near[k - low_bit]
        return exchange(from_here, "fsdp", 2 * low_bit)

    for k in range(chips):
        root = roots[k.bit_length()]
        where = k - root, tops[k.bit_length()]
        if k == 1:
            arrived, here, terms = together(arrive(1), here, terms)
            near.append(arrived)
        if k == 1 and k < last:
            arrived, here, terms = together(arrive(k + 1), here, terms)
            near.append(arrived)
        far.append(exchange(near[k], "fsdp", 1))
        common = [here, near[k], far[k], norm_gain, norm_shift]
        if k == 0:
            *made, own_normed, rstd, weights, time_held = call(
                functools.partial(first_kernel, *where, owned),
                own_shapes
                + norm_shapes
                + [
                    shape((rows, channels), f32),
                    shape((rows, channels), f32),
                    shape((9 * LANES, channels), bf16),
                    shape((owned, feature_count), bf16),
                ],
                [pltpu.VMEM(*s) for s in held] + [product, pltpu.SemaphoreType.DMA((10,))],
                16,
                1,
                2.0,
                *common,
                left=(conv_rows, time_weight),
            )
        else:
            made = call(
                functools.partial(pair_kernel, *where, owned),
                own_shapes + norm_shapes,
                [pltpu.VMEM(*s) for s in held] + [product],
                16,
                1,
                2.0,
                *common,
                weights,
                time_held,
                terms,
            )
        ours.append(list(made[:2]))
        terms = made[2]
        normed.append(list(made[3:]))
        if 1 < k < last:
            arrived, here, terms = together(arrive(k + 1), here, terms)
            near.append(arrived)

    met = [exchange(ours[k][1], "fsdp", 1) for k in range(chips)]

    def join(k):
        return call(
            join_kernel,
            shape((returned + padded, LANES), bf16 if k else f32),
            [],
            8,
            0,
            0.1,
            ours[k][0],
            met[k],
        )

    grads = [join(k) for k in range(last)]
    normed[-1][2], *grads = together(normed[-1][2], *grads)
    low, high = call(
        functools.partial(weight_grad_kernel, chips, low_taps, owned),
        (
            shape((owned, low_taps * channels + time_width), bf16),
            shape((owned, (9 - low_taps) * channels), bf16),
        ),
        [],
        min(60, 6 * chips),
        0,
        1.5,
        *(result[i] for i in range(4) for result in normed),
    )
    part, terms = call(
        join_last_kernel,
        (shape((returned + padded + TERM_ROWS, LANES), bf16), shape((TERM_ROWS, LANES), bf16)),
        [],
        8,
        0,
        0.1,
        ours[last][0],
        met[last],
        terms,
    )
    grads.append(part)

    bits = [1 << i for i in range((replicas - 1).bit_length())]
    totals = [low, high]
    early = [1, last] if last > 1 else [1]
    for step in range(len(bits)):
        orders = (bits[step], bits[-1 - step])
        received = [exchange(t, "dp", bit) for t, bit in zip(totals, orders)]
        if step == 0:
            for k in early:
                grads[k] = exchange(grads[k], "fsdp", 2 * k)
            received, grads, terms = together(received, grads, terms)
        if step < len(bits) - 1:
            totals = [
                (t.astype(f32) + r.astype(f32)).astype(bf16) for t, r in zip(totals, received)
            ]
    for k in range(1, chips):
        if k not in early:
            grads[k] = exchange(grads[k], "fsdp", 2 * k)
    terms = call(
        add_terms_kernel, shape((8, channels), f32), [], 8, 0, 0.1, terms, grads[last]
    )
    for i in range((chips - 1).bit_length() - 1):
        terms = terms + exchange(terms, "fsdp", 2 << i)
    grad_conv, grad_time = call(
        functools.partial(finish_kernel, scale),
        (shape((owned, 9 * channels), f32), shape((owned, feature_count), f32)),
        [],
        16,
        0,
        1.5,
        totals[0],
        received[0],
        totals[1],
        received[1],
    )
    block_out, grad_features = call(
        functools.partial(norm_grad_kernel, owned, chips),
        (
            shape((rows, out_channels), bf16),
            shape((rows, channels), bf16),
        ),
        [pltpu.VMEM((out_channels, rows), f32)],
        16,
        3,
        2.5,
        me,
        heights,
        widths,
        *grads,
        own_normed,
        rstd,
        norm_gain,
        norm_shift,
    )
    values = [terms] + [exchange(terms, "dp", bit) for bit in range(1, replicas)]
    grad_time, *values = together(grad_time, *values)
    while len(values) > 1:
        values = [a + b for a, b in zip(values[::2], values[1::2])]
    terms = values[0] * scale
    return (block_out, grad_features, grad_conv, grad_time, terms[0], terms[1])


def solution(mesh):
    rows = P(("dp", "fsdp"), None)
    owned = P("fsdp", None)
    return jax.shard_map(
        shards,
        mesh=mesh,
        in_specs=(rows, rows, rows, rows, P(), P(), owned, owned, rows),
        out_specs=(rows, rows, owned, owned, P(), P()),
        check_vma=False,
    )
```

```python
import functools
import math

import jax
import jax.numpy as jnp
from jax import lax
from jax.experimental import pallas as pl
from jax.experimental.pallas import tpu as pltpu
from jax.sharding import PartitionSpec as P

GROUPS = 32
IMAGES = 4
LANES = 128
TERM_ROWS = 32

bf16 = jnp.bfloat16
f32 = jnp.float32


def dot(a, b, dims=((1,), (0,))):
    return lax.dot_general(a, b, (dims, ((), ())), preferred_element_type=f32)


def split3(x):
    hi = x.astype(bf16)
    rest = x - hi.astype(f32)
    mid = rest.astype(bf16)
    low = (rest - mid.astype(f32)).astype(bf16)
    return hi, mid, low


def exact_dot(x, ones):
    rows = x.shape[0]
    out = dot(jnp.concatenate(split3(x), axis=0), ones)
    return out[:rows] + out[rows : 2 * rows] + out[2 * rows :]


def bounds_of(heights, widths):
    start = heights[0] * 0
    found = []
    for height, width in zip(heights, widths):
        area = height * width
        found.append((start, start + area, width, area))
        start = start + area
    return found


def inverse_area(area):
    return 1.0 / jnp.maximum(area, 1).astype(f32)


def masks(bounds, shape):
    row = lax.broadcasted_iota(jnp.int32, shape, 0)
    return [(row >= start) & (row < end) for start, end, _, _ in bounds]


def spread(members, table, shape):
    out = jnp.zeros(shape, f32)
    for j in range(IMAGES):
        out = jnp.where(members[j], table[j : j + 1, :], out)
    return out


def image_sums(members, values, bounds):
    sums = []
    for j in range(IMAGES):
        total = jnp.sum(jnp.where(members[j], values, 0.0), axis=0, keepdims=True)
        sums.append(total * inverse_area(bounds[j][3]))
    return jnp.concatenate(sums, axis=0)


def tap_matrices(bounds, rows):
    shape = (rows, rows)
    row = lax.broadcasted_iota(jnp.int32, shape, 0)
    gap = lax.broadcasted_iota(jnp.int32, shape, 1) - row
    width = jnp.zeros(shape, jnp.int32)
    area = jnp.zeros(shape, jnp.int32)
    first = jnp.zeros(shape, jnp.int32)
    for start, end, wide, size in bounds:
        member = (row >= start) & (row < end)
        width = jnp.where(member, wide, width)
        area = jnp.where(member, size, area)
        first = jnp.where(member, start, first)
    offset = row - first
    column = offset & (width - 1)
    columns = {-1: column >= 1, 0: column >= 0, 1: column + 1 < width}
    taps = []
    for shift_row in (-1, 0, 1):
        moved = offset + shift_row * width
        inside = (moved >= 0) & (moved < area)
        left = gap - shift_row * width
        for shift_col in (-1, 0, 1):
            hit = inside & columns[shift_col] & (left == shift_col)
            taps.append(jnp.where(hit, 1.0, 0.0).astype(bf16))
    return taps


def group_matrices(channels):
    size = channels // GROUPS
    channel = lax.broadcasted_iota(jnp.int32, (channels, LANES), 0)
    group = lax.broadcasted_iota(jnp.int32, (channels, LANES), 1)
    down = jnp.where((channel >= group * size) & (channel < (group + 1) * size), 1.0, 0.0)
    channel = lax.broadcasted_iota(jnp.int32, (LANES, channels), 1)
    group = lax.broadcasted_iota(jnp.int32, (LANES, channels), 0)
    back = jnp.where((channel >= group * size) & (channel < (group + 1) * size), 1.0, 0.0)
    return down.astype(bf16), back.astype(bf16)


def group_means(sums, matrices):
    down, back = matrices
    size = down.shape[0] // GROUPS
    return exact_dot(exact_dot(sums, down) * (1.0 / size), back)


def prepare_kernel(
    owned, me_ref, heights_ref, widths_ref, times_ref, features_ref, cotan_ref, *sent
):
    rows, channels = features_ref.shape
    holders = cotan_ref.shape[1] // owned
    padded = -(-owned // 16) * 16
    place = lax.broadcasted_iota(jnp.int32, (16, LANES), 0)
    facts = jnp.zeros((16, LANES), f32)
    for j in range(IMAGES):
        time = times_ref[0, j]
        for i, value in enumerate((heights_ref[0, j], widths_ref[0, j], time >> 5, time & 31)):
            facts = jnp.where(place == i * IMAGES + j, value.astype(f32), facts)
    facts = facts.astype(bf16)
    turned = cotan_ref[...].astype(f32).T
    chip = me_ref[0] >> 1
    slots = []
    for s in range(holders):
        part = turned[s * owned : (s + 1) * owned]
        if padded > owned:
            part = jnp.concatenate([part, jnp.zeros((padded - owned, rows), f32)], axis=0)
        slots.append(part.astype(bf16))
    first = 0
    for ref in sent:
        count = max(first, 1)
        for s in range(holders):
            slot = (chip ^ (s // 2)) - first

            @pl.when((slot >= 0) & (slot < count))
            def _():
                start = pl.multiple_of((2 * slot + s % 2) * padded, 16)
                ref[pl.ds(start, padded), :] = slots[s]

        top = count * 2 * padded
        ref[top : top + 16, :] = facts
        for q in range(channels // LANES):
            start = top + 16 + q * rows
            ref[start : start + rows, :] = features_ref[:, q * LANES : (q + 1) * LANES]
        first = max(2 * first, 1)


def chunk_sums(members, chunks, inverses):
    out = []
    for chunk in chunks:
        sums = [
            jnp.sum(jnp.where(member, chunk, 0.0), axis=0, keepdims=True) * inverse
            for member, inverse in zip(members, inverses)
        ]
        out.append(jnp.concatenate(sums, axis=0))
    return jnp.concatenate(out, axis=1)


def block_facts(ref, top):
    facts = ref[top : top + 16, :].astype(f32)
    sizes = [facts[j : j + 1, :].astype(jnp.int32) for j in range(2 * IMAGES)]
    times = facts[2 * IMAGES : 3 * IMAGES] * 32.0 + facts[3 * IMAGES :]
    return bounds_of(sizes[:IMAGES], sizes[IMAGES:]), times


def first_kernel(slot, top, owned, me_ref, near_ref, far_ref, gain_ref, shift_ref, *refs):
    conv_ref, time_ref, own_ref, other_ref, terms_ref, turned_ref, act_ref, sums_ref, embed_ref = refs[:9]
    normed_ref, rstd_ref, weights_ref, held_ref, taps, slopes, norms, product, copied = refs[9:]
    padded = conv_ref.shape[0]
    width = weights_ref.shape[1]
    copies = [pltpu.make_async_copy(time_ref, held_ref, copied.at[9])]
    for t in range(9):
        copies.append(
            pltpu.make_async_copy(
                conv_ref.at[:, pl.ds(t * width, width)],
                weights_ref.at[pl.ds(t * LANES, padded), :],
                copied.at[t],
            )
        )
        if padded < LANES:
            weights_ref[t * LANES + padded : (t + 1) * LANES, :] = jnp.zeros(
                (LANES - padded, width), bf16
            )
    for copy in copies:
        copy.start()
    blocks = me_ref, near_ref, far_ref
    norm_part(
        slot, top, time_ref.shape[1], *blocks, gain_ref, shift_ref, turned_ref, act_ref, sums_ref,
        embed_ref, taps, slopes, norms, rstd_ref,
    )
    normed_ref[...] = norms[: normed_ref.shape[0], :]
    for copy in copies:
        copy.wait()
    conv_part(
        slot, top, owned, *blocks, act_ref, embed_ref, taps, slopes, norms, weights_ref, held_ref,
        None, own_ref, other_ref, terms_ref, product,
    )


def pair_kernel(
    slot,
    top,
    owned,
    me_ref,
    near_ref,
    far_ref,
    gain_ref,
    shift_ref,
    weights_ref,
    time_ref,
    before_ref,
    own_ref,
    other_ref,
    terms_ref,
    turned_ref,
    act_ref,
    sums_ref,
    embed_ref,
    taps,
    slopes,
    norms,
    product,
):
    blocks = me_ref, near_ref, far_ref
    norm_part(
        slot, top, time_ref.shape[1], *blocks, gain_ref, shift_ref, turned_ref, act_ref, sums_ref,
        embed_ref, taps, slopes, norms, None,
    )
    conv_part(
        slot, top, owned, *blocks, act_ref, embed_ref, taps, slopes, norms, weights_ref, time_ref,
        before_ref, own_ref, other_ref, terms_ref, product,
    )


def norm_part(
    slot,
    top,
    features,
    me_ref,
    near_ref,
    far_ref,
    gain_ref,
    shift_ref,
    turned_ref,
    act_ref,
    sums_ref,
    embed_ref,
    taps_ref,
    slopes_ref,
    norms_ref,
    rstd_ref,
):
    gain = gain_ref[...].reshape(1, -1)
    shift = shift_ref[...].reshape(1, -1)
    padded = turned_ref.shape[0] // 9
    rows = LANES
    channels = act_ref.shape[1]
    count = channels // LANES
    start = pl.multiple_of((2 * slot + (me_ref[0] & 1)) * padded, 16)
    found = []
    chunks = []
    times = []
    for b, ref in enumerate((near_ref, far_ref)):
        bounds, time = block_facts(ref, top)
        times.append(time)
        taps = jnp.concatenate(tap_matrices(bounds, rows), axis=1)
        taps_ref[b * rows : (b + 1) * rows, :] = taps
        found.append((masks(bounds, (rows, LANES)), [inverse_area(size) for *_, size in bounds]))
        cotan = ref[pl.ds(start, padded), :]
        turned = dot(cotan, taps).astype(bf16)
        for t in range(9):
            turned_ref[t * padded : (t + 1) * padded, b * rows : (b + 1) * rows] = turned[
                :, t * rows : (t + 1) * rows
            ]
        image = lax.broadcasted_iota(jnp.int32, (IMAGES, rows), 0)
        place = lax.broadcasted_iota(jnp.int32, (IMAGES, rows), 1)
        member = jnp.zeros((IMAGES, rows), f32)
        for j in range(IMAGES):
            begin, end, _, _ = bounds[j]
            member = jnp.where((image == j) & (place >= begin) & (place < end), 1.0, member)
        sums_ref[b * IMAGES : (b + 1) * IMAGES, :] = dot(member.astype(bf16), cotan, ((1,), (1,)))
        first = top + 16
        chunks.append(
            [ref[first + q * rows : first + (q + 1) * rows, :].astype(f32) for q in range(count)]
        )

    matrices = group_matrices(channels)
    sums = [chunk_sums(found[b][0], chunks[b], found[b][1]) for b in range(2)]
    means = group_means(jnp.concatenate(sums, axis=0), matrices)
    sums = []
    for b in range(2):
        members, inverses = found[b]
        for q in range(count):
            mean = means[b * IMAGES : (b + 1) * IMAGES, q * LANES : (q + 1) * LANES]
            chunks[b][q] = chunks[b][q] - spread(members, mean, (rows, LANES))
        sums.append(chunk_sums(members, [c * c for c in chunks[b]], inverses))
    rstds = lax.rsqrt(group_means(jnp.concatenate(sums, axis=0), matrices) + 1e-05)
    for b in range(2):
        members = found[b][0]
        for q in range(count):
            here = slice(b * rows, (b + 1) * rows), slice(q * LANES, (q + 1) * LANES)
            rstd = rstds[b * IMAGES : (b + 1) * IMAGES, q * LANES : (q + 1) * LANES]
            rstd = spread(members, rstd, (rows, LANES))
            normed = chunks[b][q] * rstd
            shifted = normed * gain[:, here[1]] + shift[:, here[1]]
            sig = jax.nn.sigmoid(shifted)
            act_ref[here] = (shifted * sig).astype(bf16)
            slopes_ref[here] = sig * (1.0 + shifted * (1.0 - sig))
            norms_ref[here] = normed
            if rstd_ref is not None and b == 0:
                rstd_ref[:, here[1]] = rstd

    half = features // 2
    place = lax.broadcasted_iota(jnp.int32, (2 * IMAGES, half), 1).astype(f32)
    rates = jnp.exp(-math.log(10000.0) * place / half)
    angles = jnp.concatenate(times, axis=0)[:, :1] * rates
    embed_ref[...] = jnp.concatenate([jnp.sin(angles), jnp.cos(angles)], axis=1)


def conv_part(
    slot,
    top,
    owned,
    me_ref,
    near_ref,
    far_ref,
    act_ref,
    embed_ref,
    taps_ref,
    slopes_ref,
    norms_ref,
    weights_ref,
    time_ref,
    before_ref,
    own_ref,
    other_ref,
    terms_ref,
    product,
):
    rows = LANES
    channels = act_ref.shape[1]
    count = channels // LANES
    padded = own_ref.shape[0] - count * rows
    start = pl.multiple_of((2 * slot + (me_ref[0] & 1)) * padded, 16)
    weights = weights_ref[...]
    moved = []
    tiles = []
    for b, ref in enumerate((near_ref, far_ref)):
        taps = taps_ref[b * rows : (b + 1) * rows, :]
        tiles.append(taps)
        cotan = ref[pl.ds(start, padded), :]
        if padded < LANES:
            cotan = jnp.concatenate([cotan, jnp.zeros((LANES - padded, rows), bf16)], axis=0)
        stacked = [taps[:, (8 - t) * rows : (9 - t) * rows] for t in range(9)]
        shifted = dot(jnp.concatenate(stacked, axis=0), cotan, ((1,), (1,))).astype(bf16)
        moved.append(
            jnp.concatenate([shifted[t * rows : (t + 1) * rows] for t in range(9)], axis=1)
        )
    grad_act = dot(jnp.concatenate(moved, axis=0), weights)
    slope = grad_act * slopes_ref[...]
    terms = jnp.concatenate(
        [
            jnp.sum(slope * norms_ref[...], axis=0, keepdims=True),
            jnp.sum(slope, axis=0, keepdims=True),
            jnp.zeros((6, channels), f32),
        ],
        axis=0,
    )
    if before_ref is not None:
        terms = terms + before_ref[...]
    terms_ref[...] = terms
    other_ref[count * rows + padded :, :] = term_rows(terms)
    grad_act = grad_act.astype(bf16)
    product[...] = dot(act_ref[...], weights, ((1,), (1,)))
    bias = dot(embed_ref[...].astype(bf16), time_ref[...], ((1,), (1,)))
    if owned < LANES:
        bias = jnp.concatenate([bias, jnp.zeros((2 * IMAGES, LANES - owned), f32)], axis=1)
    for b, (ref, source) in enumerate(((own_ref, near_ref), (other_ref, far_ref))):
        for q in range(count):
            ref[q * rows : (q + 1) * rows, :] = grad_act[
                b * rows : (b + 1) * rows, q * LANES : (q + 1) * LANES
            ]
        values = product[b * rows : (b + 1) * rows, :]
        high = values.astype(bf16)
        low = (values - high.astype(f32)).astype(bf16)
        parts = [high[:, t * LANES : (t + 1) * LANES] for t in range(9)]
        parts += [low[:, t * LANES : (t + 1) * LANES] for t in range(9)]
        total = dot(
            jnp.concatenate([tiles[b], tiles[b]], axis=1), jnp.concatenate(parts, axis=0)
        )
        members = masks(block_facts(source, top)[0], (rows, LANES))
        total = total + spread(members, bias[b * IMAGES : (b + 1) * IMAGES], (rows, LANES))
        ref[count * rows : count * rows + padded, :] = total.T[:padded].astype(bf16)


def term_rows(terms):
    count = terms.shape[1] // LANES
    parts = [terms[r : r + 1, q * LANES : (q + 1) * LANES] for r in range(2) for q in range(count)]
    whole = jnp.concatenate(parts, axis=0)
    high = whole.astype(bf16).astype(f32)
    rest = jnp.zeros((TERM_ROWS - 4 * count, LANES), f32)
    return jnp.concatenate([high, whole - high, rest], axis=0).astype(bf16)


def terms_of(rows, channels):
    count = channels // LANES
    rows = rows.astype(f32)
    whole = rows[: 2 * count] + rows[2 * count : 4 * count]
    return jnp.concatenate(
        [
            jnp.concatenate([whole[r * count + q : r * count + q + 1] for q in range(count)], axis=1)
            for r in range(2)
        ],
        axis=0,
    )


def early_grad_kernel(pairs, *refs):
    turned, act = ([ref[...] for ref in refs[i * pairs : (i + 1) * pairs]] for i in range(2))
    refs[-1][...] = dot(jnp.concatenate(turned, axis=1), jnp.concatenate(act, axis=0))


def weight_grad_kernel(pairs, low_taps, owned, early_ref, turned_ref, act_ref, *refs):
    sums, embed = ([ref[...] for ref in refs[i * pairs : (i + 1) * pairs]] for i in range(2))
    outs = refs[2 * pairs :]

    def put(part, columns, values):
        outs[part][:, columns] = values[:owned].astype(bf16)

    channels = act_ref.shape[1]
    padded = turned_ref.shape[0] // 9
    grad = early_ref[...] + dot(turned_ref[...], act_ref[...])
    for t in range(9):
        part, place = (0, t) if t < low_taps else (1, t - low_taps)
        columns = slice(place * channels, (place + 1) * channels)
        put(part, columns, grad[t * padded : (t + 1) * padded])
    embed = jnp.concatenate(embed, axis=0).astype(bf16)
    time_grad = jnp.zeros((padded, embed.shape[1]), f32)
    for term in split3(jnp.concatenate(sums, axis=0)):
        time_grad = time_grad + dot(term, embed, ((0,), (0,)))
    width = outs[0].shape[1]
    spare = width - low_taps * channels - embed.shape[1]
    time_grad = jnp.concatenate([time_grad, jnp.zeros((padded, spare), f32)], axis=1)
    put(0, slice(low_taps * channels, width), time_grad)


def join_kernel(own_ref, met_ref, out_ref):
    size = own_ref.shape[0]
    top = 2 * size - out_ref.shape[0]
    total = own_ref[:top, :].astype(f32) + met_ref[:top, :].astype(f32)
    out_ref[:top, :] = total.astype(out_ref.dtype)
    out_ref[top:size, :] = own_ref[top:, :].astype(out_ref.dtype)
    out_ref[size:, :] = met_ref[top:size, :].astype(out_ref.dtype)


def join_last_kernel(own_ref, met_ref, terms_ref, out_ref, sums_ref):
    join_kernel(own_ref, met_ref, out_ref.at[: out_ref.shape[0] - TERM_ROWS, :])
    channels = terms_ref.shape[1]
    mine = terms_of(term_rows(terms_ref[...]), channels)
    terms = term_rows(mine + terms_of(met_ref[-TERM_ROWS:, :], channels))
    out_ref[out_ref.shape[0] - TERM_ROWS :, :] = terms
    sums_ref[...] = terms


def add_terms_kernel(terms_ref, met_ref, out_ref):
    channels = out_ref.shape[1]
    total = terms_of(terms_ref[...], channels) + terms_of(met_ref[-TERM_ROWS:, :], channels)
    out_ref[...] = jnp.concatenate([total, jnp.zeros((6, channels), f32)], axis=0)


def norm_grad_kernel(
    owned,
    chips,
    me_ref,
    heights_ref,
    widths_ref,
    *refs,
):
    terms = refs[:chips]
    normed_ref, rstd_ref, gain_ref, shift_ref, out_ref, grad_ref, joined = refs[chips:]
    rows, channels = rstd_ref.shape
    top = channels // LANES * rows
    padded = (terms[0].shape[0] - top) // 2
    end = top + 2 * padded
    me = me_ref[0]
    pieces = []
    for ref in terms:
        pieces += [ref[top : top + padded, :], ref[top + padded : end, :]]
    for b, piece in enumerate(pieces):
        start = pl.multiple_of((me ^ b) * owned, 8)
        joined[pl.ds(start, owned), :] = piece[:owned].astype(f32)
    out_ref[...] = joined[...].T.astype(bf16)

    total = terms[0][:top, :]
    for ref in terms[1:]:
        total = total + ref[:top, :].astype(f32)
    total = jnp.concatenate(
        [total[q * rows : (q + 1) * rows] for q in range(channels // LANES)], axis=1
    )
    normed = normed_ref[...]
    gain = gain_ref[...].reshape(1, -1)
    shifted = normed * gain + shift_ref[...].reshape(1, -1)
    sig = jax.nn.sigmoid(shifted)
    slope = total * (sig * (1.0 + shifted * (1.0 - sig)))
    grad = slope * gain
    bounds = bounds_of(
        [heights_ref[0, j] for j in range(IMAGES)], [widths_ref[0, j] for j in range(IMAGES)]
    )
    members = masks(bounds, (rows, channels))
    sums = jnp.concatenate(
        [image_sums(members, grad, bounds), image_sums(members, grad * normed, bounds)], axis=0
    )
    means = group_means(sums, group_matrices(channels))
    mean_grad = spread(members, means[:IMAGES], (rows, channels))
    mean_cross = spread(members, means[IMAGES:], (rows, channels))
    grad_ref[...] = (rstd_ref[...] * (grad - mean_grad - normed * mean_cross)).astype(bf16)


def finish_kernel(scale, low_ref, low_met_ref, high_ref, high_met_ref, *refs):
    conv_ref, time_ref, gain_ref, shift_ref = refs[-4:]
    values = [ref[...] for ref in refs[:-4]]
    while len(values) > 1:
        values = [a + b for a, b in zip(values[::2], values[1::2])]
    gain_ref[...] = (values[0][0:1, :] * scale).reshape(-1)
    shift_ref[...] = (values[0][1:2, :] * scale).reshape(-1)
    low = (low_ref[...].astype(f32) + low_met_ref[...].astype(f32)) * scale
    width = conv_ref.shape[1] - high_ref.shape[1]
    conv_ref[:, :width] = low[:, :width]
    time_ref[...] = low[:, width : width + time_ref.shape[1]]
    conv_ref[:, width:] = (high_ref[...].astype(f32) + high_met_ref[...].astype(f32)) * scale


def call(kernel, outs, scratch, limit, scalars, microseconds, *args, left=()):
    smem = pl.BlockSpec(memory_space=pltpu.SMEM)
    vmem = pl.BlockSpec(memory_space=pltpu.VMEM)
    return pl.pallas_call(
        kernel,
        out_shape=outs,
        in_specs=[smem] * scalars
        + [vmem] * (len(args) - scalars)
        + [pl.BlockSpec(memory_space=pl.ANY)] * len(left),
        out_specs=jax.tree.map(lambda _: vmem, outs),
        scratch_shapes=scratch,
        compiler_params=pltpu.CompilerParams(vmem_limit_bytes=limit << 20),
        cost_estimate=pl.CostEstimate(
            flops=int(microseconds * 0.5 * 1e9),
            bytes_accessed=int(microseconds * 0.5 * 3e6),
            transcendentals=0,
        ),
    )(*args, *left)


def exchange(value, axis, bit):
    size = lax.axis_size(axis)
    return lax.ppermute(value, axis, [(i, i ^ bit) for i in range(size)])


def together(*values):
    return lax.optimization_barrier(values)


def shards(
    features, heights, widths, timesteps, norm_gain, norm_shift, conv_weight, time_weight, cotangent
):
    rows, channels = features.shape
    replicas = lax.axis_size("dp")
    holders = lax.axis_size("fsdp")
    chips = holders // 2
    owned = conv_weight.shape[0]
    out_channels = cotangent.shape[1]
    feature_count = time_weight.shape[1]
    scale = 1.0 / math.sqrt(replicas * holders * rows)
    me = lax.axis_index("fsdp").astype(jnp.int32)[None]
    padded = -(-owned // 16) * 16
    low_taps = 4
    time_width = -(-feature_count // LANES) * LANES
    shape = jax.ShapeDtypeStruct

    roots = [0] + [1 << i for i in range((chips - 1).bit_length())]
    tops = [2 * padded * max(root, 1) for root in roots]
    sent = call(
        functools.partial(prepare_kernel, owned),
        [shape((top + 16 + channels // LANES * rows, LANES), bf16) for top in tops],
        [],
        60,
        4,
        4.0,
        me,
        heights,
        widths,
        timesteps,
        features,
        cotangent,
    )
    returned = channels // LANES * rows + padded
    last = chips - 1
    if padded > owned:
        conv_rows = jnp.pad(conv_weight, ((0, padded - owned), (0, 0)))
    else:
        conv_rows = conv_weight
    own_shapes = [
        shape((returned, LANES), bf16),
        shape((returned + TERM_ROWS, LANES), bf16),
        shape((8, channels), f32),
    ]
    norm_shapes = [
        shape((9 * padded, 2 * rows), bf16),
        shape((2 * rows, channels), bf16),
        shape((2 * IMAGES, padded), f32),
        shape((2 * IMAGES, feature_count), f32),
    ]
    held = [
        ((2 * rows, 9 * rows), bf16),
        ((2 * rows, channels), f32),
        ((2 * rows, channels), f32),
    ]
    product = pltpu.VMEM((2 * rows, 9 * LANES), f32)

    near, far, ours, normed = [sent[0]], [], [], []
    here = me

    def arrive(k):
        low_bit = k & -k
        from_here = sent[k.bit_length()] if k == low_bit else near[k - low_bit]
        return exchange(from_here, "fsdp", 2 * low_bit)

    for k in range(chips):
        root = roots[k.bit_length()]
        where = k - root, tops[k.bit_length()]
        if k == 1:
            arrived, here, terms = together(arrive(1), here, terms)
            near.append(arrived)
        if k == 1 and k < last:
            arrived, here, terms = together(arrive(k + 1), here, terms)
            near.append(arrived)
        far.append(exchange(near[k], "fsdp", 1))
        common = [here, near[k], far[k], norm_gain, norm_shift]
        if k == 0:
            *made, own_normed, rstd, weights, time_held = call(
                functools.partial(first_kernel, *where, owned),
                own_shapes
                + norm_shapes
                + [
                    shape((rows, channels), f32),
                    shape((rows, channels), f32),
                    shape((9 * LANES, channels), bf16),
                    shape((owned, feature_count), bf16),
                ],
                [pltpu.VMEM(*s) for s in held] + [product, pltpu.SemaphoreType.DMA((10,))],
                16,
                1,
                2.0,
                *common,
                left=(conv_rows, time_weight),
            )
        else:
            made = call(
                functools.partial(pair_kernel, *where, owned),
                own_shapes + norm_shapes,
                [pltpu.VMEM(*s) for s in held] + [product],
                16,
                1,
                2.0,
                *common,
                weights,
                time_held,
                terms,
            )
        ours.append(list(made[:2]))
        terms = made[2]
        normed.append(list(made[3:]))
        if 1 < k < last:
            arrived, here, terms, normed[0][0] = together(
                arrive(k + 1), here, terms, normed[0][0]
            )
            near.append(arrived)
        if k == last - 1:
            early = call(
                functools.partial(early_grad_kernel, last),
                shape((9 * padded, channels), f32),
                [],
                min(60, 6 * chips),
                0,
                1.0,
                *(result[i] for i in range(2) for result in normed),
            )
            here, early = together(here, early)

    met = [exchange(ours[k][1], "fsdp", 1) for k in range(chips)]

    def join(k):
        return call(
            join_kernel,
            shape((returned + padded, LANES), bf16 if k else f32),
            [],
            8,
            0,
            0.1,
            ours[k][0],
            met[k],
        )

    grads = [join(k) for k in range(last)]
    normed[-1][2], *grads = together(normed[-1][2], *grads)
    low, high = call(
        functools.partial(weight_grad_kernel, chips, low_taps, owned),
        (
            shape((owned, low_taps * channels + time_width), bf16),
            shape((owned, (9 - low_taps) * channels), bf16),
        ),
        [],
        min(60, 6 * chips),
        0,
        1.0,
        early,
        *normed[last][:2],
        *(result[i] for i in (2, 3) for result in normed),
    )
    part, terms = call(
        join_last_kernel,
        (shape((returned + padded + TERM_ROWS, LANES), bf16), shape((TERM_ROWS, LANES), bf16)),
        [],
        8,
        0,
        0.1,
        ours[last][0],
        met[last],
        terms,
    )
    grads.append(part)

    bits = [1 << i for i in range((replicas - 1).bit_length())]
    totals = [low, high]
    firsts = [1, last] if last > 1 else [1]
    for step in range(len(bits)):
        orders = (bits[step], bits[-1 - step])
        received = [exchange(t, "dp", bit) for t, bit in zip(totals, orders)]
        if step == 0:
            for k in firsts:
                grads[k] = exchange(grads[k], "fsdp", 2 * k)
            received, grads, terms = together(received, grads, terms)
        if step < len(bits) - 1:
            totals = [
                (t.astype(f32) + r.astype(f32)).astype(bf16) for t, r in zip(totals, received)
            ]
    for k in range(1, chips):
        if k not in firsts:
            grads[k] = exchange(grads[k], "fsdp", 2 * k)
    terms = call(
        add_terms_kernel, shape((8, channels), f32), [], 8, 0, 0.1, terms, grads[last]
    )
    for i in range((chips - 1).bit_length() - 1):
        terms = terms + exchange(terms, "fsdp", 2 << i)
    block_out, grad_features = call(
        functools.partial(norm_grad_kernel, owned, chips),
        (
            shape((rows, out_channels), bf16),
            shape((rows, channels), bf16),
        ),
        [pltpu.VMEM((out_channels, rows), f32)],
        16,
        3,
        2.5,
        me,
        heights,
        widths,
        *grads,
        own_normed,
        rstd,
        norm_gain,
        norm_shift,
    )
    values = [terms] + [exchange(terms, "dp", bit) for bit in range(1, replicas)]
    grad_conv, grad_time, grad_gain, grad_shift = call(
        functools.partial(finish_kernel, scale),
        (shape((owned, 9 * channels), f32), shape((owned, feature_count), f32))
        + (shape((channels,), f32),) * 2,
        [],
        16,
        0,
        1.5,
        totals[0],
        received[0],
        totals[1],
        received[1],
        *values,
    )
    return (block_out, grad_features, grad_conv, grad_time, grad_gain, grad_shift)


def solution(mesh):
    rows = P(("dp", "fsdp"), None)
    owned = P("fsdp", None)
    return jax.shard_map(
        shards,
        mesh=mesh,
        in_specs=(rows, rows, rows, rows, P(), P(), owned, owned, rows),
        out_specs=(rows, rows, owned, owned, P(), P()),
        check_vma=False,
    )
```

```python
import functools
import math

import jax
import jax.numpy as jnp
from jax import lax
from jax.experimental import pallas as pl
from jax.experimental.pallas import tpu as pltpu
from jax.sharding import PartitionSpec as P

GROUPS = 32
IMAGES = 4
LANES = 128
TERM_ROWS = 32

bf16 = jnp.bfloat16
f32 = jnp.float32


def dot(a, b, dims=((1,), (0,))):
    return lax.dot_general(a, b, (dims, ((), ())), preferred_element_type=f32)


def split3(x):
    hi = x.astype(bf16)
    rest = x - hi.astype(f32)
    mid = rest.astype(bf16)
    low = (rest - mid.astype(f32)).astype(bf16)
    return hi, mid, low


def exact_dot(x, ones):
    rows = x.shape[0]
    out = dot(jnp.concatenate(split3(x), axis=0), ones)
    return out[:rows] + out[rows : 2 * rows] + out[2 * rows :]


def bounds_of(heights, widths):
    start = heights[0] * 0
    found = []
    for height, width in zip(heights, widths):
        area = height * width
        found.append((start, start + area, width, area))
        start = start + area
    return found


def inverse_area(area):
    return 1.0 / jnp.maximum(area, 1).astype(f32)


def masks(bounds, shape):
    row = lax.broadcasted_iota(jnp.int32, shape, 0)
    return [(row >= start) & (row < end) for start, end, _, _ in bounds]


def spread(members, table, shape):
    out = jnp.zeros(shape, f32)
    for j in range(IMAGES):
        out = jnp.where(members[j], table[j : j + 1, :], out)
    return out


def image_sums(members, values, bounds):
    sums = []
    for j in range(IMAGES):
        total = jnp.sum(jnp.where(members[j], values, 0.0), axis=0, keepdims=True)
        sums.append(total * inverse_area(bounds[j][3]))
    return jnp.concatenate(sums, axis=0)


def tap_matrices(bounds, rows):
    shape = (rows, rows)
    row = lax.broadcasted_iota(jnp.int32, shape, 0)
    gap = lax.broadcasted_iota(jnp.int32, shape, 1) - row
    width = jnp.zeros(shape, jnp.int32)
    area = jnp.zeros(shape, jnp.int32)
    first = jnp.zeros(shape, jnp.int32)
    for start, end, wide, size in bounds:
        member = (row >= start) & (row < end)
        width = jnp.where(member, wide, width)
        area = jnp.where(member, size, area)
        first = jnp.where(member, start, first)
    offset = row - first
    column = offset & (width - 1)
    columns = {-1: column >= 1, 0: column >= 0, 1: column + 1 < width}
    taps = []
    for shift_row in (-1, 0, 1):
        moved = offset + shift_row * width
        inside = (moved >= 0) & (moved < area)
        left = gap - shift_row * width
        for shift_col in (-1, 0, 1):
            hit = inside & columns[shift_col] & (left == shift_col)
            taps.append(jnp.where(hit, 1.0, 0.0).astype(bf16))
    return taps


def group_matrices(channels):
    size = channels // GROUPS
    channel = lax.broadcasted_iota(jnp.int32, (channels, LANES), 0)
    group = lax.broadcasted_iota(jnp.int32, (channels, LANES), 1)
    down = jnp.where((channel >= group * size) & (channel < (group + 1) * size), 1.0, 0.0)
    channel = lax.broadcasted_iota(jnp.int32, (LANES, channels), 1)
    group = lax.broadcasted_iota(jnp.int32, (LANES, channels), 0)
    back = jnp.where((channel >= group * size) & (channel < (group + 1) * size), 1.0, 0.0)
    return down.astype(bf16), back.astype(bf16)


def group_means(sums, matrices):
    down, back = matrices
    size = down.shape[0] // GROUPS
    return exact_dot(exact_dot(sums, down) * (1.0 / size), back)


def prepare_kernel(
    owned, me_ref, heights_ref, widths_ref, times_ref, features_ref, cotan_ref, *sent
):
    rows, channels = features_ref.shape
    holders = cotan_ref.shape[1] // owned
    padded = -(-owned // 16) * 16
    place = lax.broadcasted_iota(jnp.int32, (16, LANES), 0)
    facts = jnp.zeros((16, LANES), f32)
    for j in range(IMAGES):
        time = times_ref[0, j]
        for i, value in enumerate((heights_ref[0, j], widths_ref[0, j], time >> 5, time & 31)):
            facts = jnp.where(place == i * IMAGES + j, value.astype(f32), facts)
    facts = facts.astype(bf16)
    turned = cotan_ref[...].astype(f32).T
    chip = me_ref[0] >> 1
    slots = []
    for s in range(holders):
        part = turned[s * owned : (s + 1) * owned]
        if padded > owned:
            part = jnp.concatenate([part, jnp.zeros((padded - owned, rows), f32)], axis=0)
        slots.append(part.astype(bf16))
    first = 0
    for ref in sent:
        count = max(first, 1)
        for s in range(holders):
            slot = (chip ^ (s // 2)) - first

            @pl.when((slot >= 0) & (slot < count))
            def _():
                start = pl.multiple_of((2 * slot + s % 2) * padded, 16)
                ref[pl.ds(start, padded), :] = slots[s]

        top = count * 2 * padded
        ref[top : top + 16, :] = facts
        for q in range(channels // LANES):
            start = top + 16 + q * rows
            ref[start : start + rows, :] = features_ref[:, q * LANES : (q + 1) * LANES]
        first = max(2 * first, 1)


def chunk_sums(members, chunks, inverses):
    out = []
    for chunk in chunks:
        sums = [
            jnp.sum(jnp.where(member, chunk, 0.0), axis=0, keepdims=True) * inverse
            for member, inverse in zip(members, inverses)
        ]
        out.append(jnp.concatenate(sums, axis=0))
    return jnp.concatenate(out, axis=1)


def block_facts(ref, top):
    facts = ref[top : top + 16, :].astype(f32)
    sizes = [facts[j : j + 1, :].astype(jnp.int32) for j in range(2 * IMAGES)]
    times = facts[2 * IMAGES : 3 * IMAGES] * 32.0 + facts[3 * IMAGES :]
    return bounds_of(sizes[:IMAGES], sizes[IMAGES:]), times


def first_kernel(slot, top, owned, me_ref, near_ref, far_ref, gain_ref, shift_ref, *refs):
    conv_ref, time_ref, own_ref, other_ref, terms_ref, turned_ref, act_ref, sums_ref, embed_ref = refs[:9]
    normed_ref, rstd_ref, weights_ref, held_ref, taps, slopes, norms, product, copied = refs[9:]
    padded = conv_ref.shape[0]
    width = weights_ref.shape[1]
    copies = [pltpu.make_async_copy(time_ref, held_ref, copied.at[9])]
    for t in range(9):
        copies.append(
            pltpu.make_async_copy(
                conv_ref.at[:, pl.ds(t * width, width)],
                weights_ref.at[pl.ds(t * LANES, padded), :],
                copied.at[t],
            )
        )
        if padded < LANES:
            weights_ref[t * LANES + padded : (t + 1) * LANES, :] = jnp.zeros(
                (LANES - padded, width), bf16
            )
    for copy in copies:
        copy.start()
    blocks = me_ref, near_ref, far_ref
    norm_part(
        slot, top, time_ref.shape[1], *blocks, gain_ref, shift_ref, turned_ref, act_ref, sums_ref,
        embed_ref, taps, slopes, norms, rstd_ref,
    )
    normed_ref[...] = norms[: normed_ref.shape[0], :]
    for copy in copies:
        copy.wait()
    conv_part(
        slot, top, owned, *blocks, act_ref, embed_ref, taps, slopes, norms, weights_ref, held_ref,
        None, own_ref, other_ref, terms_ref, product,
    )


def pair_kernel(
    slot,
    top,
    owned,
    me_ref,
    near_ref,
    far_ref,
    gain_ref,
    shift_ref,
    weights_ref,
    time_ref,
    before_ref,
    own_ref,
    other_ref,
    terms_ref,
    turned_ref,
    act_ref,
    sums_ref,
    embed_ref,
    taps,
    slopes,
    norms,
    product,
):
    blocks = me_ref, near_ref, far_ref
    norm_part(
        slot, top, time_ref.shape[1], *blocks, gain_ref, shift_ref, turned_ref, act_ref, sums_ref,
        embed_ref, taps, slopes, norms, None,
    )
    conv_part(
        slot, top, owned, *blocks, act_ref, embed_ref, taps, slopes, norms, weights_ref, time_ref,
        before_ref, own_ref, other_ref, terms_ref, product,
    )


def norm_part(
    slot,
    top,
    features,
    me_ref,
    near_ref,
    far_ref,
    gain_ref,
    shift_ref,
    turned_ref,
    act_ref,
    sums_ref,
    embed_ref,
    taps_ref,
    slopes_ref,
    norms_ref,
    rstd_ref,
):
    gain = gain_ref[...].reshape(1, -1)
    shift = shift_ref[...].reshape(1, -1)
    padded = turned_ref.shape[0] // 9
    rows = LANES
    channels = act_ref.shape[1]
    count = channels // LANES
    start = pl.multiple_of((2 * slot + (me_ref[0] & 1)) * padded, 16)
    found = []
    chunks = []
    times = []
    for b, ref in enumerate((near_ref, far_ref)):
        bounds, time = block_facts(ref, top)
        times.append(time)
        taps = jnp.concatenate(tap_matrices(bounds, rows), axis=1)
        taps_ref[b * rows : (b + 1) * rows, :] = taps
        found.append((masks(bounds, (rows, LANES)), [inverse_area(size) for *_, size in bounds]))
        cotan = ref[pl.ds(start, padded), :]
        turned = dot(cotan, taps).astype(bf16)
        for t in range(9):
            turned_ref[t * padded : (t + 1) * padded, b * rows : (b + 1) * rows] = turned[
                :, t * rows : (t + 1) * rows
            ]
        image = lax.broadcasted_iota(jnp.int32, (IMAGES, rows), 0)
        place = lax.broadcasted_iota(jnp.int32, (IMAGES, rows), 1)
        member = jnp.zeros((IMAGES, rows), f32)
        for j in range(IMAGES):
            begin, end, _, _ = bounds[j]
            member = jnp.where((image == j) & (place >= begin) & (place < end), 1.0, member)
        sums_ref[b * IMAGES : (b + 1) * IMAGES, :] = dot(member.astype(bf16), cotan, ((1,), (1,)))
        first = top + 16
        chunks.append(
            [ref[first + q * rows : first + (q + 1) * rows, :].astype(f32) for q in range(count)]
        )

    matrices = group_matrices(channels)
    sums = [chunk_sums(found[b][0], chunks[b], found[b][1]) for b in range(2)]
    means = group_means(jnp.concatenate(sums, axis=0), matrices)
    sums = []
    for b in range(2):
        members, inverses = found[b]
        for q in range(count):
            mean = means[b * IMAGES : (b + 1) * IMAGES, q * LANES : (q + 1) * LANES]
            chunks[b][q] = chunks[b][q] - spread(members, mean, (rows, LANES))
        sums.append(chunk_sums(members, [c * c for c in chunks[b]], inverses))
    rstds = lax.rsqrt(group_means(jnp.concatenate(sums, axis=0), matrices) + 1e-05)
    for b in range(2):
        members = found[b][0]
        for q in range(count):
            here = slice(b * rows, (b + 1) * rows), slice(q * LANES, (q + 1) * LANES)
            rstd = rstds[b * IMAGES : (b + 1) * IMAGES, q * LANES : (q + 1) * LANES]
            rstd = spread(members, rstd, (rows, LANES))
            normed = chunks[b][q] * rstd
            shifted = normed * gain[:, here[1]] + shift[:, here[1]]
            sig = jax.nn.sigmoid(shifted)
            act_ref[here] = (shifted * sig).astype(bf16)
            slopes_ref[here] = sig * (1.0 + shifted * (1.0 - sig))
            norms_ref[here] = normed
            if rstd_ref is not None and b == 0:
                rstd_ref[:, here[1]] = rstd

    half = features // 2
    place = lax.broadcasted_iota(jnp.int32, (2 * IMAGES, half), 1).astype(f32)
    rates = jnp.exp(-math.log(10000.0) * place / half)
    angles = jnp.concatenate(times, axis=0)[:, :1] * rates
    embed_ref[...] = jnp.concatenate([jnp.sin(angles), jnp.cos(angles)], axis=1)


def conv_part(
    slot,
    top,
    owned,
    me_ref,
    near_ref,
    far_ref,
    act_ref,
    embed_ref,
    taps_ref,
    slopes_ref,
    norms_ref,
    weights_ref,
    time_ref,
    before_ref,
    own_ref,
    other_ref,
    terms_ref,
    product,
):
    rows = LANES
    channels = act_ref.shape[1]
    count = channels // LANES
    padded = own_ref.shape[0] - count * rows
    start = pl.multiple_of((2 * slot + (me_ref[0] & 1)) * padded, 16)
    weights = weights_ref[...]
    moved = []
    tiles = []
    for b, ref in enumerate((near_ref, far_ref)):
        taps = taps_ref[b * rows : (b + 1) * rows, :]
        tiles.append(taps)
        cotan = ref[pl.ds(start, padded), :]
        if padded < LANES:
            cotan = jnp.concatenate([cotan, jnp.zeros((LANES - padded, rows), bf16)], axis=0)
        stacked = [taps[:, (8 - t) * rows : (9 - t) * rows] for t in range(9)]
        shifted = dot(jnp.concatenate(stacked, axis=0), cotan, ((1,), (1,))).astype(bf16)
        moved.append(
            jnp.concatenate([shifted[t * rows : (t + 1) * rows] for t in range(9)], axis=1)
        )
    grad_act = dot(jnp.concatenate(moved, axis=0), weights)
    slope = grad_act * slopes_ref[...]
    terms = jnp.concatenate(
        [
            jnp.sum(slope * norms_ref[...], axis=0, keepdims=True),
            jnp.sum(slope, axis=0, keepdims=True),
            jnp.zeros((6, channels), f32),
        ],
        axis=0,
    )
    if before_ref is not None:
        terms = terms + before_ref[...]
    terms_ref[...] = terms
    other_ref[count * rows + padded :, :] = term_rows(terms)
    grad_act = grad_act.astype(bf16)
    product[...] = dot(act_ref[...], weights, ((1,), (1,)))
    bias = dot(embed_ref[...].astype(bf16), time_ref[...], ((1,), (1,)))
    if owned < LANES:
        bias = jnp.concatenate([bias, jnp.zeros((2 * IMAGES, LANES - owned), f32)], axis=1)
    for b, (ref, source) in enumerate(((own_ref, near_ref), (other_ref, far_ref))):
        for q in range(count):
            ref[q * rows : (q + 1) * rows, :] = grad_act[
                b * rows : (b + 1) * rows, q * LANES : (q + 1) * LANES
            ]
        values = product[b * rows : (b + 1) * rows, :]
        high = values.astype(bf16)
        low = (values - high.astype(f32)).astype(bf16)
        parts = [high[:, t * LANES : (t + 1) * LANES] for t in range(9)]
        parts += [low[:, t * LANES : (t + 1) * LANES] for t in range(9)]
        total = dot(
            jnp.concatenate([tiles[b], tiles[b]], axis=1), jnp.concatenate(parts, axis=0)
        )
        members = masks(block_facts(source, top)[0], (rows, LANES))
        total = total + spread(members, bias[b * IMAGES : (b + 1) * IMAGES], (rows, LANES))
        ref[count * rows : count * rows + padded, :] = total.T[:padded].astype(bf16)


def term_rows(terms):
    count = terms.shape[1] // LANES
    parts = [terms[r : r + 1, q * LANES : (q + 1) * LANES] for r in range(2) for q in range(count)]
    whole = jnp.concatenate(parts, axis=0)
    high = whole.astype(bf16).astype(f32)
    rest = jnp.zeros((TERM_ROWS - 4 * count, LANES), f32)
    return jnp.concatenate([high, whole - high, rest], axis=0).astype(bf16)


def terms_of(rows, channels):
    count = channels // LANES
    rows = rows.astype(f32)
    whole = rows[: 2 * count] + rows[2 * count : 4 * count]
    return jnp.concatenate(
        [
            jnp.concatenate([whole[r * count + q : r * count + q + 1] for q in range(count)], axis=1)
            for r in range(2)
        ],
        axis=0,
    )


def early_grad_kernel(pairs, *refs):
    turned, act = ([ref[...] for ref in refs[i * pairs : (i + 1) * pairs]] for i in range(2))
    refs[-1][...] = dot(jnp.concatenate(turned, axis=1), jnp.concatenate(act, axis=0))


def weight_grad_kernel(pairs, low_taps, owned, early_ref, turned_ref, act_ref, *refs):
    sums, embed = ([ref[...] for ref in refs[i * pairs : (i + 1) * pairs]] for i in range(2))
    outs = refs[2 * pairs :]

    def put(part, columns, values):
        outs[part][:, columns] = values[:owned].astype(bf16)

    channels = act_ref.shape[1]
    padded = turned_ref.shape[0] // 9
    grad = early_ref[...] + dot(turned_ref[...], act_ref[...])
    for t in range(9):
        part, place = (0, t) if t < low_taps else (1, t - low_taps)
        columns = slice(place * channels, (place + 1) * channels)
        put(part, columns, grad[t * padded : (t + 1) * padded])
    embed = jnp.concatenate(embed, axis=0).astype(bf16)
    time_grad = jnp.zeros((padded, embed.shape[1]), f32)
    for term in split3(jnp.concatenate(sums, axis=0)):
        time_grad = time_grad + dot(term, embed, ((0,), (0,)))
    width = outs[0].shape[1]
    spare = width - low_taps * channels - embed.shape[1]
    time_grad = jnp.concatenate([time_grad, jnp.zeros((padded, spare), f32)], axis=1)
    put(0, slice(low_taps * channels, width), time_grad)


def join_kernel(own_ref, met_ref, out_ref):
    size = own_ref.shape[0]
    top = 2 * size - out_ref.shape[0]
    total = own_ref[:top, :].astype(f32) + met_ref[:top, :].astype(f32)
    out_ref[:top, :] = total.astype(out_ref.dtype)
    out_ref[top:size, :] = own_ref[top:, :].astype(out_ref.dtype)
    out_ref[size:, :] = met_ref[top:size, :].astype(out_ref.dtype)


def join_last_kernel(own_ref, met_ref, terms_ref, out_ref, sums_ref):
    join_kernel(own_ref, met_ref, out_ref.at[: out_ref.shape[0] - TERM_ROWS, :])
    channels = terms_ref.shape[1]
    mine = terms_of(term_rows(terms_ref[...]), channels)
    terms = term_rows(mine + terms_of(met_ref[-TERM_ROWS:, :], channels))
    out_ref[out_ref.shape[0] - TERM_ROWS :, :] = terms
    sums_ref[...] = terms


def add_terms_kernel(terms_ref, met_ref, out_ref):
    channels = out_ref.shape[1]
    total = terms_of(terms_ref[...], channels) + terms_of(met_ref[-TERM_ROWS:, :], channels)
    out_ref[...] = jnp.concatenate([total, jnp.zeros((6, channels), f32)], axis=0)


def norm_grad_kernel(
    owned,
    chips,
    me_ref,
    heights_ref,
    widths_ref,
    *refs,
):
    terms = refs[:chips]
    normed_ref, rstd_ref, gain_ref, shift_ref, out_ref, grad_ref, joined = refs[chips:]
    rows, channels = rstd_ref.shape
    top = channels // LANES * rows
    padded = (terms[0].shape[0] - top) // 2
    end = top + 2 * padded
    me = me_ref[0]
    pieces = []
    for ref in terms:
        pieces += [ref[top : top + padded, :], ref[top + padded : end, :]]
    for b, piece in enumerate(pieces):
        start = pl.multiple_of((me ^ b) * owned, 8)
        joined[pl.ds(start, owned), :] = piece[:owned].astype(f32)
    out_ref[...] = joined[...].T.astype(bf16)

    total = terms[0][:top, :]
    for ref in terms[1:]:
        total = total + ref[:top, :].astype(f32)
    total = jnp.concatenate(
        [total[q * rows : (q + 1) * rows] for q in range(channels // LANES)], axis=1
    )
    normed = normed_ref[...]
    gain = gain_ref[...].reshape(1, -1)
    shifted = normed * gain + shift_ref[...].reshape(1, -1)
    sig = jax.nn.sigmoid(shifted)
    slope = total * (sig * (1.0 + shifted * (1.0 - sig)))
    grad = slope * gain
    bounds = bounds_of(
        [heights_ref[0, j] for j in range(IMAGES)], [widths_ref[0, j] for j in range(IMAGES)]
    )
    members = masks(bounds, (rows, channels))
    sums = jnp.concatenate(
        [image_sums(members, grad, bounds), image_sums(members, grad * normed, bounds)], axis=0
    )
    means = group_means(sums, group_matrices(channels))
    mean_grad = spread(members, means[:IMAGES], (rows, channels))
    mean_cross = spread(members, means[IMAGES:], (rows, channels))
    grad_ref[...] = (rstd_ref[...] * (grad - mean_grad - normed * mean_cross)).astype(bf16)


def finish_kernel(scale, low_ref, low_met_ref, high_ref, high_met_ref, *refs):
    conv_ref, time_ref, gain_ref, shift_ref = refs[-4:]
    values = [ref[...] for ref in refs[:-4]]
    while len(values) > 1:
        values = [a + b for a, b in zip(values[::2], values[1::2])]
    gain_ref[...] = (values[0][0:1, :] * scale).reshape(-1)
    shift_ref[...] = (values[0][1:2, :] * scale).reshape(-1)
    low = (low_ref[...].astype(f32) + low_met_ref[...].astype(f32)) * scale
    width = conv_ref.shape[1] - high_ref.shape[1]
    conv_ref[:, :width] = low[:, :width]
    time_ref[...] = low[:, width : width + time_ref.shape[1]]
    conv_ref[:, width:] = (high_ref[...].astype(f32) + high_met_ref[...].astype(f32)) * scale


def call(kernel, outs, scratch, limit, scalars, microseconds, *args, left=()):
    smem = pl.BlockSpec(memory_space=pltpu.SMEM)
    vmem = pl.BlockSpec(memory_space=pltpu.VMEM)
    return pl.pallas_call(
        kernel,
        out_shape=outs,
        in_specs=[smem] * scalars
        + [vmem] * (len(args) - scalars)
        + [pl.BlockSpec(memory_space=pl.ANY)] * len(left),
        out_specs=jax.tree.map(lambda _: vmem, outs),
        scratch_shapes=scratch,
        compiler_params=pltpu.CompilerParams(vmem_limit_bytes=limit << 20),
        cost_estimate=pl.CostEstimate(
            flops=int(microseconds * 0.5 * 1e9),
            bytes_accessed=int(microseconds * 0.5 * 3e6),
            transcendentals=0,
        ),
    )(*args, *left)


def exchange(value, axis, bit):
    size = lax.axis_size(axis)
    return lax.ppermute(value, axis, [(i, i ^ bit) for i in range(size)])


def together(*values):
    return lax.optimization_barrier(values)


def shards(
    features, heights, widths, timesteps, norm_gain, norm_shift, conv_weight, time_weight, cotangent
):
    rows, channels = features.shape
    replicas = lax.axis_size("dp")
    holders = lax.axis_size("fsdp")
    chips = holders // 2
    owned = conv_weight.shape[0]
    out_channels = cotangent.shape[1]
    feature_count = time_weight.shape[1]
    scale = 1.0 / math.sqrt(replicas * holders * rows)
    me = lax.axis_index("fsdp").astype(jnp.int32)[None]
    padded = -(-owned // 16) * 16
    low_taps = 4
    time_width = -(-feature_count // LANES) * LANES
    shape = jax.ShapeDtypeStruct

    roots = [0] + [1 << i for i in range((chips - 1).bit_length())]
    tops = [2 * padded * max(root, 1) for root in roots]
    sent = call(
        functools.partial(prepare_kernel, owned),
        [shape((top + 16 + channels // LANES * rows, LANES), bf16) for top in tops],
        [],
        60,
        4,
        4.0,
        me,
        heights,
        widths,
        timesteps,
        features,
        cotangent,
    )
    returned = channels // LANES * rows + padded
    last = chips - 1
    if padded > owned:
        conv_rows = jnp.pad(conv_weight, ((0, padded - owned), (0, 0)))
    else:
        conv_rows = conv_weight
    own_shapes = [
        shape((returned, LANES), bf16),
        shape((returned + TERM_ROWS, LANES), bf16),
        shape((8, channels), f32),
    ]
    norm_shapes = [
        shape((9 * padded, 2 * rows), bf16),
        shape((2 * rows, channels), bf16),
        shape((2 * IMAGES, padded), f32),
        shape((2 * IMAGES, feature_count), f32),
    ]
    held = [
        ((2 * rows, 9 * rows), bf16),
        ((2 * rows, channels), f32),
        ((2 * rows, channels), f32),
    ]
    product = pltpu.VMEM((2 * rows, 9 * LANES), f32)

    near, far, ours, normed = [sent[0]], [], [], []
    here = me

    def arrive(k):
        low_bit = k & -k
        from_here = sent[k.bit_length()] if k == low_bit else near[k - low_bit]
        return exchange(from_here, "fsdp", 2 * low_bit)

    for k in range(chips):
        root = roots[k.bit_length()]
        where = k - root, tops[k.bit_length()]
        if k == 1:
            arrived, here, terms = together(arrive(1), here, terms)
            near.append(arrived)
        if k == 1 and k < last:
            arrived, here, terms = together(arrive(k + 1), here, terms)
            near.append(arrived)
        far.append(exchange(near[k], "fsdp", 1))
        common = [here, near[k], far[k], norm_gain, norm_shift]
        if k == 0:
            *made, own_normed, rstd, weights, time_held = call(
                functools.partial(first_kernel, *where, owned),
                own_shapes
                + norm_shapes
                + [
                    shape((rows, channels), f32),
                    shape((rows, channels), f32),
                    shape((9 * LANES, channels), bf16),
                    shape((owned, feature_count), bf16),
                ],
                [pltpu.VMEM(*s) for s in held] + [product, pltpu.SemaphoreType.DMA((10,))],
                16,
                1,
                2.0,
                *common,
                left=(conv_rows, time_weight),
            )
        else:
            made = call(
                functools.partial(pair_kernel, *where, owned),
                own_shapes + norm_shapes,
                [pltpu.VMEM(*s) for s in held] + [product],
                16,
                1,
                2.0,
                *common,
                weights,
                time_held,
                terms,
            )
        ours.append(list(made[:2]))
        terms = made[2]
        normed.append(list(made[3:]))
        if 1 < k < last:
            arrived, here, terms, normed[0][0] = together(
                arrive(k + 1), here, terms, normed[0][0]
            )
            near.append(arrived)
        if k == last - 1:
            early = call(
                functools.partial(early_grad_kernel, last),
                shape((9 * padded, channels), f32),
                [],
                min(60, 6 * chips),
                0,
                1.0,
                *(result[i] for i in range(2) for result in normed),
            )
            here, early = together(here, early)

    met = [exchange(ours[k][1], "fsdp", 1) for k in range(chips)]

    def join(k):
        return call(
            join_kernel,
            shape((returned + padded, LANES), bf16 if k else f32),
            [],
            8,
            0,
            0.1,
            ours[k][0],
            met[k],
        )

    grads = [join(k) for k in range(last)]
    normed[-1][2], *grads = together(normed[-1][2], *grads)
    part, terms = call(
        join_last_kernel,
        (shape((returned + padded + TERM_ROWS, LANES), bf16), shape((TERM_ROWS, LANES), bf16)),
        [],
        8,
        0,
        0.1,
        ours[last][0],
        met[last],
        terms,
    )
    normed[last][2], part, terms = together(normed[last][2], part, terms)
    low, high = call(
        functools.partial(weight_grad_kernel, chips, low_taps, owned),
        (
            shape((owned, low_taps * channels + time_width), bf16),
            shape((owned, (9 - low_taps) * channels), bf16),
        ),
        [],
        min(60, 6 * chips),
        0,
        1.0,
        early,
        *normed[last][:2],
        *(result[i] for i in (2, 3) for result in normed),
    )
    grads.append(part)

    bits = [1 << i for i in range((replicas - 1).bit_length())]
    totals = [low, high]
    firsts = [1, last] if last > 1 else [1]
    for step in range(len(bits)):
        orders = (bits[step], bits[-1 - step])
        received = [exchange(t, "dp", bit) for t, bit in zip(totals, orders)]
        if step == 0:
            for k in firsts:
                grads[k] = exchange(grads[k], "fsdp", 2 * k)
            received, grads, terms = together(received, grads, terms)
        if step < len(bits) - 1:
            totals = [
                (t.astype(f32) + r.astype(f32)).astype(bf16) for t, r in zip(totals, received)
            ]
    for k in range(1, chips):
        if k not in firsts:
            grads[k] = exchange(grads[k], "fsdp", 2 * k)
    terms = call(
        add_terms_kernel, shape((8, channels), f32), [], 8, 0, 0.1, terms, grads[last]
    )
    for i in range((chips - 1).bit_length() - 1):
        terms = terms + exchange(terms, "fsdp", 2 << i)
    block_out, grad_features = call(
        functools.partial(norm_grad_kernel, owned, chips),
        (
            shape((rows, out_channels), bf16),
            shape((rows, channels), bf16),
        ),
        [pltpu.VMEM((out_channels, rows), f32)],
        16,
        3,
        2.5,
        me,
        heights,
        widths,
        *grads,
        own_normed,
        rstd,
        norm_gain,
        norm_shift,
    )
    values = [terms] + [exchange(terms, "dp", bit) for bit in range(1, replicas)]
    grad_conv, grad_time, grad_gain, grad_shift = call(
        functools.partial(finish_kernel, scale),
        (shape((owned, 9 * channels), f32), shape((owned, feature_count), f32))
        + (shape((channels,), f32),) * 2,
        [],
        16,
        0,
        1.5,
        totals[0],
        received[0],
        totals[1],
        received[1],
        *values,
    )
    return (block_out, grad_features, grad_conv, grad_time, grad_gain, grad_shift)


def solution(mesh):
    rows = P(("dp", "fsdp"), None)
    owned = P("fsdp", None)
    return jax.shard_map(
        shards,
        mesh=mesh,
        in_specs=(rows, rows, rows, rows, P(), P(), owned, owned, rows),
        out_specs=(rows, rows, owned, owned, P(), P()),
        check_vma=False,
    )
```
